32 devices in a mesh: grid: 4 (over y, x), dom: 8 (over z, core).
Axes of the slice: x: 2, y: 2, z: 4, core: 2. Of those that a mesh axis runs over, the one named last changes fastest.
Arguments:
- state_field: float32 [4, 16, 8, 16384], P('grid', 'dom'), may hold values from -6 to 6
- level_vectors: int32 [4, 4], P('grid'), may hold values from 2 to 5, as said below
- combine_weights: int32 [4], P('grid'), may hold values from -2 to 2, as said below
- diffusion: float32 [6], replicated, may hold values from 0.05 to 0.08
- courant: float32 [6], replicated, may hold values from -0.3 to 0.3
Outputs:
- combined_field: float32 [4, 16, 8, 16384], P('grid', 'dom')
The draws below stay inside these ranges and needn't reach their ends.
Inputs may be any that keep to these rules, and one draw needn't show every extreme that they name: `level_vectors`: each row holds 2, 3, 4, 5 in some order. `combine_weights`: never zero.
All inputs are finite; a program needn't handle non-finite values.
Results may differ from the reference program's by a relative error of at most 0.0003.
Values sent between devices are 32-bit elements; how exact they have to be, the bound alone decides.
A program may use at most 128 MiB of HBM per device.

```python
import jax
import jax.numpy as jnp
from jax import lax

SECOND = 8
LOW = 2
LOCAL = 16384
NX = 16
GRIDS = 4


def draw_level_vectors(key, part):
    scores = jax.random.randint(jax.random.fold_in(key, 11), (GRIDS, 4), 0, 1024) * 4 + jnp.arange(4, dtype=jnp.int32)[None, :]
    ordering = jnp.argsort(scores, axis=1, stable=True).astype(jnp.int32)
    return (ordering + LOW).astype(jnp.int32)


def draw_combine_weights(key, part):
    picks = jax.random.randint(jax.random.fold_in(key, 23), (GRIDS,), 0, 4)
    return (picks - 2 + (picks >= 2).astype(jnp.int32)).astype(jnp.int32)


def level_of(own_key, shape, split, smallest, top_value):
    def one(position, blocks):
        steps = jax.random.uniform(jax.random.fold_in(jax.random.fold_in(own_key, 6), position), (blocks,), jnp.float32, smallest / len(split), top_value / len(split))
        return jnp.repeat(jnp.exp(steps), shape[position] // blocks).reshape((-1,) + (1,) * (len(shape) - position - 1))

    loudness = one(*split[0])
    for cut in split[1:]:
        loudness = loudness * one(*cut)
    return loudness


def bell_draw(rng, dims, deviation, bound, shards=(), kind=jnp.bfloat16):
    drawn = deviation * jax.random.normal(rng, dims, jnp.float32)
    if shards:
        drawn = drawn * level_of(rng, dims, shards, -0.22, 0.18)
    return jnp.clip(drawn, -bound, bound).astype(kind)


def setup_inputs(seed: int = 0) -> dict:
    keys = jax.random.split(jax.random.key(seed), 6)
    state_field = bell_draw(keys[0], (GRIDS, NX, SECOND, LOCAL), 1.0, 6.0, ((0, 4), (1, 8)), jnp.float32)
    level_vectors = draw_level_vectors(jax.random.fold_in(keys[5], 71), 0)
    combine_weights = draw_combine_weights(jax.random.fold_in(keys[5], 71), 0)
    diffusion = jnp.clip(jax.random.uniform(keys[3], (6,), jnp.float32, 0.05, 0.08), 0.05, 0.08)
    courant = jnp.clip(jax.random.uniform(keys[4], (6,), jnp.float32, -0.3, 0.3), -0.3, 0.3)
    return dict(state_field=state_field, level_vectors=level_vectors, combine_weights=combine_weights, diffusion=diffusion, courant=courant)


def level_pass(values, dimension, spacing, orientation):
    length = values.shape[dimension]
    parents = lax.slice_in_dim(values, 0, length, 2 * spacing, dimension)
    beside = jnp.roll(parents, -1, dimension)
    selector = [slice(None)] * values.ndim
    selector[dimension] = slice(spacing, length, 2 * spacing)
    return values.at[tuple(selector)].add(orientation * 0.5 * (parents + beside))


def spacings(length, orientation):
    ladder = [2 ** exponent for exponent in range(length.bit_length() - 1)]
    return ladder if orientation < 0 else ladder[::-1]


def sweep(values, dimensions, orientation):
    for dimension in dimensions:
        for spacing in spacings(values.shape[dimension], orientation):
            values = level_pass(values, dimension, spacing, orientation)
    return values


def local_shape(row_count, second_len):
    return (row_count, second_len, 2 ** LOW, 2 ** (LOW + 1), 2 ** (LOW + 2), 2 ** (LOW + 3))


def stencil_numbers(level_row, diffusion, courant):
    matches = (level_row[:, None] == (LOW + jnp.arange(4, dtype=jnp.int32))[None, :]).astype(jnp.float32)
    local_diff = jnp.sum(diffusion[2:, None] * matches, axis=0)
    local_cour = jnp.sum(courant[2:, None] * matches, axis=0)
    return jnp.concatenate([diffusion[:2], local_diff]), jnp.concatenate([courant[:2], local_cour])


def stencil_update(center, forward_rows, backward_rows, diff_num, cour_num):
    update = diff_num[0] * (forward_rows + backward_rows - 2.0 * center) - 0.5 * cour_num[0] * (forward_rows - backward_rows)
    for dimension in range(1, 6):
        forward = jnp.roll(center, -1, dimension)
        backward = jnp.roll(center, 1, dimension)
        update = update + diff_num[dimension] * (forward + backward - 2.0 * center) - 0.5 * cour_num[dimension] * (forward - backward)
    return center + update


def subspace_map(level_row):
    side_len = 2 ** LOW
    entries = side_len ** 4
    flat_ids = jnp.arange(entries, dtype=jnp.int32)
    target = jnp.zeros((entries,), jnp.int32)
    for physical in range(4):
        digits = (flat_ids // side_len ** (3 - physical)) % side_len
        stored = (level_row[physical] - LOW).astype(jnp.int32)
        target = target + digits * jnp.power(side_len, 3 - stored).astype(jnp.int32)
    return (flat_ids[:, None] == target[None, :]).astype(jnp.float32)


def reference(state_field, level_vectors, combine_weights, diffusion, courant):
    nodes = state_field.shape[1]
    side_len = 2 ** LOW
    hierarchized = []
    projected = []
    for member in range(GRIDS):
        diff_num, cour_num = stencil_numbers(level_vectors[member], diffusion, courant)
        values = state_field[member].reshape(local_shape(nodes, SECOND))
        for repeat in range(2):
            values = stencil_update(values, jnp.roll(values, -1, 0), jnp.roll(values, 1, 0), diff_num, cour_num)
        values = sweep(values, [2, 3, 4, 5], -1.0)
        mapping = subspace_map(level_vectors[member])
        shared = values[:, :, :, ::2, ::4, ::8].reshape(nodes * SECOND, side_len ** 4)
        weighted = combine_weights[member].astype(jnp.float32) * jnp.dot(shared, mapping, precision=lax.Precision.HIGHEST)
        projected.append(weighted)
        hierarchized.append(values)
    combined = projected[0]
    for weighted in projected[1:]:
        combined = combined + weighted
    results = []
    for member in range(GRIDS):
        mapping = subspace_map(level_vectors[member])
        returned = jnp.dot(combined, mapping.T, precision=lax.Precision.HIGHEST)
        values = hierarchized[member].at[:, :, :, ::2, ::4, ::8].set(returned.reshape(nodes, SECOND, side_len, side_len, side_len, side_len))
        values = sweep(values, [2, 3, 4, 5], 1.0)
        results.append(values.reshape(nodes, SECOND, -1))
    return jnp.stack(results)
```

```python
import functools

import jax
import jax.numpy as jnp
import numpy as np
from jax import lax
from jax.experimental import pallas as pl
from jax.experimental.pallas import tpu as pltpu
from jax.sharding import PartitionSpec as P

LOW = 2
SIDE = 2**LOW
COARSE = SIDE**4
LANES = 128
GROUP = 16 * SIDE * SIDE * 2
MESH = pl.DeviceIdType.MESH


def level_matrix(length, orientation):
    ladder = [2**e for e in range(length.bit_length() - 1)]
    total = np.eye(length)
    for h in ladder if orientation < 0 else ladder[::-1]:
        step = np.eye(length)
        for i in range(h, length, 2 * h):
            step[i, (i - h) % length] += 0.5 * orientation
            step[i, (i + h) % length] += 0.5 * orientation
        total = step @ total
    return total


def kron4(m):
    return np.kron(np.kron(np.kron(m, m), m), m)


def packed_order():
    p = np.arange(COARSE)
    tile = p // LANES * 32 + p % LANES // 32 * 8 + p % 8
    return tile * 4 + p % 32 // 8


def interpolation(ratio):
    fine = np.arange(ratio * SIDE)
    gap = (fine[None, :] - ratio * np.arange(SIDE)[:, None]) % (ratio * SIDE)
    reach = np.minimum(gap, ratio * SIDE - gap)
    return np.maximum(1.0 - reach / ratio, 0.0)


def constant_table():
    down = kron4(level_matrix(SIDE, -1.0)).T[packed_order()]
    up = kron4(level_matrix(SIDE, 1.0)).T
    spread = np.kron(interpolation(4), interpolation(8))
    spread = np.tile(spread, (COARSE // spread.shape[0], 1))
    return np.concatenate([down, up, spread], axis=1).astype(jnp.bfloat16)


def parts_of(x):
    high = x.astype(jnp.bfloat16)
    rest = x - high.astype(jnp.float32)
    mid = rest.astype(jnp.bfloat16)
    low = (rest - mid.astype(jnp.float32)).astype(jnp.bfloat16)
    return high, mid, low


def exact_dot(x, table):
    high, mid, low = parts_of(x)
    dot = functools.partial(jnp.dot, preferred_element_type=jnp.float32)
    return dot(high, table) + (dot(mid, table) + dot(low, table))


def kernel(
    grids, doms, chunks,
    level_ref, weight_ref, diff_ref, cour_ref, state_ref, table_hbm,
    out_ref,
    u, w, acc, near, far, mine, table, c_out, c_in, g_out, g_in, z,
    in_sem, raw_s, raw_r, far_s, far_r, cs, cr, gs, gr, out_sem,
):
    rows, second, cells = u.shape
    gi, di = lax.axis_index("grid"), lax.axis_index("dom")
    above, below = lax.rem(di + 1, doms), lax.rem(di + doms - 1, doms)
    peers = [lax.rem(gi + k, grids) for k in range(1, grids)]

    barrier = pltpu.get_barrier_semaphore()
    for side in (above, below):
        pl.semaphore_signal(barrier, inc=1, device_id=(gi, side), device_id_type=MESH)
    for peer in peers:
        pl.semaphore_signal(barrier, inc=1, device_id=(peer, di), device_id_type=MESH)
    load = pltpu.make_async_copy(state_ref.at[0], u, in_sem.at[0])
    load.start()
    load_table = pltpu.make_async_copy(table_hbm, table, in_sem.at[1])
    load_table.start()
    pl.semaphore_wait(barrier, 2 + len(peers))

    targets = ((gi, above), (gi, below))
    raw = []
    for s, row in ((0, rows - 1), (1, 0)):
        raw.append(
            pltpu.make_async_remote_copy(
                src_ref=state_ref.at[0, row], dst_ref=near.at[s],
                send_sem=raw_s.at[s], recv_sem=raw_r.at[s],
                device_id=targets[s], device_id_type=MESH,
            )
        )
        raw[-1].start()

    kappa, sigma = [diff_ref[0], diff_ref[1]], [cour_ref[0], cour_ref[1]]
    for j in range(4):
        k_sum, s_sum = jnp.float32(0.0), jnp.float32(0.0)
        for p in range(4):
            here = level_ref[0, p] == LOW + j
            k_sum = k_sum + jnp.where(here, diff_ref[2 + p], 0.0)
            s_sum = s_sum + jnp.where(here, cour_ref[2 + p], 0.0)
        kappa.append(k_sum)
        sigma.append(s_sum)
    a = [k - 0.5 * s for k, s in zip(kappa, sigma)]
    b = [k + 0.5 * s for k, s in zip(kappa, sigma)]
    centre = 1.0 - 2.0 * (kappa[0] + kappa[1] + kappa[2] + kappa[3] + kappa[4] + kappa[5])

    lane = lax.broadcasted_iota(jnp.int32, (second, LANES), 1)
    digit = lane % 32
    first_digit, last_digit = digit == 0, digit == 31
    in_low, in_high = lane < LANES - 32, lane >= 32
    tiles = GROUP // LANES
    outer = cells // GROUP
    n3 = 2 * SIDE
    n2 = outer // n3

    def neighbours(g):
        d2, d3 = g // n3, g % n3
        starts = []
        for e2, e3 in ((1, 0), (n2 - 1, 0), (0, 1), (0, n3 - 1)):
            starts.append(((d2 + e2) % n2 * n3 + (d3 + e3) % n3) * GROUP)
        return starts

    def apply_d(ref, r, g):
        here = g * GROUP
        n = neighbours(g)
        at = lambda start, t: ref[r, :, pl.ds(pl.multiple_of(start + t * LANES, LANES), LANES)]
        v = [at(here, t) for t in range(tiles)]
        ahead = [pltpu.roll(x, LANES - 32, 1) for x in v]
        behind = [pltpu.roll(x, 32, 1) for x in v]
        out = []
        for t, x in enumerate(v):
            y = centre * x
            y += a[1] * pltpu.roll(x, second - 1, 0) + b[1] * pltpu.roll(x, 1, 0)
            y += a[2] * at(n[0], t) + b[2] * at(n[1], t)
            y += a[3] * at(n[2], t) + b[3] * at(n[3], t)
            y += a[4] * jnp.where(in_low, ahead[t], ahead[(t + 1) % tiles])
            y += b[4] * jnp.where(in_high, behind[t], behind[(t - 1) % tiles])
            y += a[5] * jnp.where(last_digit, pltpu.roll(x, 31, 1), pltpu.roll(x, LANES - 1, 1))
            y += b[5] * jnp.where(first_digit, pltpu.roll(x, LANES - 31, 1), pltpu.roll(x, 1, 1))
            out.append(y)
        return v, out

    def spot(g, t):
        return pl.ds(pl.multiple_of(g * GROUP + t * LANES, LANES), LANES)

    load.wait()

    @pl.loop(0, outer)
    def _(g):
        us, ws = [], []
        for r in range(rows):
            v, y = apply_d(u, r, g)
            us.append(v)
            ws.append(y)
            for t in range(tiles):
                w[r, :, spot(g, t)] = y[t]
        for t in range(tiles):
            mine[0, :, spot(g, t)] = 2.0 * b[0] * ws[rows - 1][t] + b[0] * b[0] * us[rows - 2][t]
            mine[1, :, spot(g, t)] = 2.0 * a[0] * ws[0][t] + a[0] * a[0] * us[1][t]

    coarse_lane = (lane < 32) & (lane % 8 == 0)

    def pack(ref, r):
        halves = []
        for half in range(2):
            total = None
            for block in range(4):
                part = None
                for k in range(8):
                    i = half * 32 + block * 8 + k
                    start = (i // 16 * n3 + i // 4 % 4 * 2) * GROUP + i % 4 * LANES
                    x = jnp.where(coarse_lane, ref[r, :, start : start + LANES], 0.0)
                    x = x if k == 0 else pltpu.roll(x, k, 1)
                    part = x if part is None else part + x
                part = part if block == 0 else pltpu.roll(part, 32 * block, 1)
                total = part if total is None else total + part
            halves.append(total)
        return halves

    def store_pack(dst, slot, place, ref, r):
        low, high = pack(ref, r)
        dst[slot, place, :, 0:LANES] = low
        dst[slot, place, :, LANES : 2 * LANES] = high

    store_pack(c_out, 0, 0, u, rows - 1)
    store_pack(c_out, 0, 1, mine, 0)
    store_pack(c_out, 1, 0, u, 0)
    store_pack(c_out, 1, 1, mine, 1)

    coarse, bulk = [], []
    for s in range(2):
        coarse.append(
            pltpu.make_async_remote_copy(
                src_ref=c_out.at[s], dst_ref=c_in.at[s],
                send_sem=cs.at[s], recv_sem=cr.at[s],
                device_id=targets[s], device_id_type=MESH,
            )
        )
        coarse[-1].start()
    width = cells // chunks
    for c in range(chunks):
        for s in range(2):
            cut = (s, slice(None), pl.ds(c * width, width))
            bulk.append(
                pltpu.make_async_remote_copy(
                    src_ref=mine.at[cut], dst_ref=far.at[cut],
                    send_sem=far_s.at[s, c], recv_sem=far_r.at[s, c],
                    device_id=targets[s], device_id_type=MESH,
                )
            )
            bulk[-1].start()

    @pl.loop(0, outer)
    def _(g):
        for r in range(rows):
            _, y = apply_d(w, r, g)
            for t in range(tiles):
                x = y[t] + 2.0 * a[0] * b[0] * u[r, :, spot(g, t)]
                if r + 1 < rows:
                    x += 2.0 * a[0] * w[r + 1, :, spot(g, t)]
                if r >= 1:
                    x += 2.0 * b[0] * w[r - 1, :, spot(g, t)]
                if r + 2 < rows:
                    x += a[0] * a[0] * u[r + 2, :, spot(g, t)]
                if r >= 2:
                    x += b[0] * b[0] * u[r - 2, :, spot(g, t)]
                acc[r, :, spot(g, t)] = x

    scale = []
    for p in range(4):
        value = jnp.int32(0)
        for j in range(4):
            value = value + jnp.where(level_ref[0, p] == LOW + j, SIDE ** (3 - j), 0)
        scale.append(value)

    def placement(flat):
        target = jnp.zeros_like(flat)
        for p in range(4):
            target = target + flat // SIDE ** (3 - p) % SIDE * scale[p]
        return target

    row_id = lax.broadcasted_iota(jnp.int32, (COARSE, COARSE), 0)
    col_id = lax.broadcasted_iota(jnp.int32, (COARSE, COARSE), 1)
    one = lambda hit: jnp.where(hit, 1.0, 0.0).astype(jnp.bfloat16)
    forward = one(row_id == placement(col_id))
    backward = one(col_id == placement(row_id))

    pieces = [jnp.concatenate(pack(acc, r), axis=1) for r in range(rows)]
    for s in range(2):
        coarse[s].wait_recv()
    pieces[0] += c_in[0, 1]
    pieces[1] += b[0] * b[0] * c_in[0, 0]
    pieces[rows - 1] += c_in[1, 1]
    pieces[rows - 2] += a[0] * a[0] * c_in[1, 0]
    points = jnp.concatenate(pieces, axis=0)
    load_table.wait()
    surplus = exact_dot(points, table[:, 0:COARSE])
    weighted = weight_ref[0].astype(jnp.float32) * exact_dot(surplus, forward)
    g_out[...] = weighted
    shares = []
    for k, peer in enumerate(peers):
        shares.append(
            pltpu.make_async_remote_copy(
                src_ref=g_out, dst_ref=g_in.at[k],
                send_sem=gs.at[k], recv_sem=gr.at[k],
                device_id=(peer, di), device_id_type=MESH,
            )
        )
        shares[-1].start()
    combined = weighted
    for k in range(len(peers)):
        shares[k].wait_recv()
        combined = combined + g_in[k]
    change = exact_dot(combined, backward) - surplus
    change = exact_dot(change, table[:, COARSE : 2 * COARSE])

    per_group = 16
    for g in range(COARSE // per_group):
        half, place = g * per_group // LANES, g % (LANES // per_group)
        x = change[:, half * LANES : (half + 1) * LANES]
        block = lax.broadcasted_iota(jnp.int32, x.shape, 1) // per_group
        x = jnp.where(block == place, x, 0.0)
        z[g] = exact_dot(x, table[0:LANES, 2 * COARSE :])

    for s in range(2):
        raw[s].wait_recv()

    @pl.loop(0, outer // 2)
    def _(i):
        d2, c3 = i // SIDE, i % SIDE
        after = d2 * SIDE + (c3 + 1) % SIDE
        for r in range(rows):
            for t in range(tiles):
                cut = (pl.ds(r * second, second), slice(t * LANES, (t + 1) * LANES))
                even = z[(i,) + cut]
                odd = 0.5 * (even + z[(after,) + cut])
                for h, x in ((0, even), (1, odd)):
                    if r == 1:
                        x += b[0] * b[0] * near[0, :, spot(2 * i + h, t)]
                    if r == rows - 2:
                        x += a[0] * a[0] * near[1, :, spot(2 * i + h, t)]
                    acc[r, :, spot(2 * i + h, t)] += x

    saves = []
    for c in range(chunks):
        for s in range(2):
            bulk[2 * c + s].wait_recv()

        @pl.loop(0, width // GROUP)
        def _(i):
            for t in range(tiles):
                here = spot(c * (width // GROUP) + i, t)
                acc[0, :, here] += far[0, :, here]
                acc[rows - 1, :, here] += far[1, :, here]

        cut = (slice(None), slice(None), pl.ds(c * width, width))
        saves.append(pltpu.make_async_copy(acc.at[cut], out_ref.at[(0,) + cut], out_sem.at[c]))
        saves[-1].start()
    for copy in raw + coarse + bulk + shares:
        copy.wait_send()
    for copy in saves:
        copy.wait()


def local(grids, doms, state_field, level_vectors, combine_weights, diffusion, courant):
    _, rows, second, cells = state_field.shape
    chunks = 4
    table = jnp.asarray(constant_table())
    f32 = jnp.float32
    dma = pltpu.SemaphoreType.DMA
    smem = pl.BlockSpec(memory_space=pltpu.SMEM)
    anywhere = pl.BlockSpec(memory_space=pl.ANY)
    others = max(grids - 1, 1)
    return pl.pallas_call(
        functools.partial(kernel, grids, doms, chunks),
        out_shape=jax.ShapeDtypeStruct(state_field.shape, f32),
        in_specs=[smem] * 4 + [anywhere] * 2,
        out_specs=anywhere,
        scratch_shapes=[
            pltpu.VMEM((rows, second, cells), f32),
            pltpu.VMEM((rows, second, cells), f32),
            pltpu.VMEM((rows, second, cells), f32),
            pltpu.VMEM((2, second, cells), f32),
            pltpu.VMEM((2, second, cells), f32),
            pltpu.VMEM((2, second, cells), f32),
            pltpu.VMEM(table.shape, jnp.bfloat16),
            pltpu.VMEM((2, 2, second, COARSE), f32),
            pltpu.VMEM((2, 2, second, COARSE), f32),
            pltpu.VMEM((rows * second, COARSE), f32),
            pltpu.VMEM((others, rows * second, COARSE), f32),
            pltpu.VMEM((SIDE * SIDE, rows * second, GROUP), f32),
            dma((2,)),
            dma((2,)),
            dma((2,)),
            dma((2, chunks)),
            dma((2, chunks)),
            dma((2,)),
            dma((2,)),
            dma((others,)),
            dma((others,)),
            dma((chunks,)),
        ],
        compiler_params=pltpu.CompilerParams(
            collective_id=0, has_side_effects=True, vmem_limit_bytes=40 * 2**20
        ),
    )(level_vectors, combine_weights, diffusion, courant, state_field, table)


def solution(mesh):
    placed = (P("grid", "dom", None, None), P("grid", None), P("grid"), P(), P())
    return jax.shard_map(
        functools.partial(local, mesh.shape["grid"], mesh.shape["dom"]),
        mesh=mesh,
        in_specs=placed,
        out_specs=P("grid", "dom", None, None),
        check_vma=False,
    )
```

```python
import functools

import jax
import jax.numpy as jnp
import numpy as np
from jax import lax
from jax.experimental import pallas as pl
from jax.experimental.pallas import tpu as pltpu
from jax.sharding import PartitionSpec as P

LOW = 2
SIDE = 2**LOW
COARSE = SIDE**4
LANES = 128
GROUP = 16 * SIDE * SIDE * 2
MESH = pl.DeviceIdType.MESH


def level_matrix(length, orientation):
    ladder = [2**e for e in range(length.bit_length() - 1)]
    total = np.eye(length)
    for h in ladder if orientation < 0 else ladder[::-1]:
        step = np.eye(length)
        for i in range(h, length, 2 * h):
            step[i, (i - h) % length] += 0.5 * orientation
            step[i, (i + h) % length] += 0.5 * orientation
        total = step @ total
    return total


def kron4(m):
    return np.kron(np.kron(np.kron(m, m), m), m)


def packed_order():
    p = np.arange(COARSE)
    tile = p // LANES * 32 + p % LANES // 32 * 8 + p % 8
    return tile * 4 + p % 32 // 8


def interpolation(ratio):
    fine = np.arange(ratio * SIDE)
    gap = (fine[None, :] - ratio * np.arange(SIDE)[:, None]) % (ratio * SIDE)
    reach = np.minimum(gap, ratio * SIDE - gap)
    return np.maximum(1.0 - reach / ratio, 0.0)


def constant_table():
    down = kron4(level_matrix(SIDE, -1.0)).T[packed_order()]
    up = kron4(level_matrix(SIDE, 1.0)).T[:, packed_order()]
    spread = np.kron(interpolation(4), interpolation(8))
    spread = spread[packed_order()[:LANES] % spread.shape[0]]
    spread = np.concatenate([spread, spread], axis=0)
    return np.concatenate([down, up, spread], axis=1).astype(jnp.bfloat16)


def parts_of(x):
    high = x.astype(jnp.bfloat16)
    rest = x - high.astype(jnp.float32)
    mid = rest.astype(jnp.bfloat16)
    low = (rest - mid.astype(jnp.float32)).astype(jnp.bfloat16)
    return high, mid, low


def exact_dot(x, table):
    n = x.shape[0]
    y = jnp.dot(jnp.concatenate(parts_of(x), axis=0), table, preferred_element_type=jnp.float32)
    return y[0:n] + (y[n : 2 * n] + y[2 * n : 3 * n])


def kernel(
    grids, doms, chunks,
    level_ref, weight_ref, diff_ref, cour_ref, state_ref, table_hbm,
    out_ref,
    u, w, acc, near, far, mine, table, c_out, c_in, g_out, g_in, z,
    in_sem, raw_s, raw_r, far_s, far_r, cs, cr, gs, gr, out_sem,
):
    rows, second, cells = u.shape
    gi, di = lax.axis_index("grid"), lax.axis_index("dom")
    above, below = lax.rem(di + 1, doms), lax.rem(di + doms - 1, doms)
    peers = [lax.rem(gi + k, grids) for k in range(1, grids)]

    barrier = pltpu.get_barrier_semaphore()
    for side in (above, below):
        pl.semaphore_signal(barrier, inc=1, device_id=(gi, side), device_id_type=MESH)
    for peer in peers:
        pl.semaphore_signal(barrier, inc=1, device_id=(peer, di), device_id_type=MESH)
    load = pltpu.make_async_copy(state_ref.at[0], u, in_sem.at[0])
    load.start()
    load_table = pltpu.make_async_copy(table_hbm, table, in_sem.at[1])
    load_table.start()
    pl.semaphore_wait(barrier, 2 + len(peers))

    targets = ((gi, above), (gi, below))
    raw = []
    for s, row in ((0, rows - 1), (1, 0)):
        raw.append(
            pltpu.make_async_remote_copy(
                src_ref=state_ref.at[0, row], dst_ref=near.at[s],
                send_sem=raw_s.at[s], recv_sem=raw_r.at[s],
                device_id=targets[s], device_id_type=MESH,
            )
        )
        raw[-1].start()

    kappa, sigma = [diff_ref[0], diff_ref[1]], [cour_ref[0], cour_ref[1]]
    for j in range(4):
        k_sum, s_sum = jnp.float32(0.0), jnp.float32(0.0)
        for p in range(4):
            here = level_ref[0, p] == LOW + j
            k_sum = k_sum + jnp.where(here, diff_ref[2 + p], 0.0)
            s_sum = s_sum + jnp.where(here, cour_ref[2 + p], 0.0)
        kappa.append(k_sum)
        sigma.append(s_sum)
    a = [k - 0.5 * s for k, s in zip(kappa, sigma)]
    b = [k + 0.5 * s for k, s in zip(kappa, sigma)]
    centre = 1.0 - 2.0 * (kappa[0] + kappa[1] + kappa[2] + kappa[3] + kappa[4] + kappa[5])

    lane = lax.broadcasted_iota(jnp.int32, (second, LANES), 1)
    digit = lane % 32
    first_digit, last_digit = digit == 0, digit == 31
    in_low, in_high = lane < LANES - 32, lane >= 32
    tiles = GROUP // LANES
    outer = cells // GROUP
    n3 = 2 * SIDE

    def neighbours(g):
        base, low = g & ~(n3 - 1), n3 - 1
        ids = [(g + n3) & (outer - 1), (g - n3) & (outer - 1)]
        ids += [base | ((g + 1) & low), base | ((g - 1) & low)]
        return [i * GROUP for i in ids]

    def apply_d(ref, r, g):
        here = g * GROUP
        n = neighbours(g)
        at = lambda start, t: ref[r, :, pl.ds(pl.multiple_of(start + t * LANES, LANES), LANES)]
        v = [at(here, t) for t in range(tiles)]
        ahead = [pltpu.roll(x, LANES - 32, 1) for x in v]
        behind = [pltpu.roll(x, 32, 1) for x in v]
        out = []
        for t, x in enumerate(v):
            y = centre * x
            y += a[1] * pltpu.roll(x, second - 1, 0) + b[1] * pltpu.roll(x, 1, 0)
            y += a[2] * at(n[0], t) + b[2] * at(n[1], t)
            y += a[3] * at(n[2], t) + b[3] * at(n[3], t)
            y += a[4] * jnp.where(in_low, ahead[t], ahead[(t + 1) % tiles])
            y += b[4] * jnp.where(in_high, behind[t], behind[(t - 1) % tiles])
            y += a[5] * jnp.where(last_digit, pltpu.roll(x, 31, 1), pltpu.roll(x, LANES - 1, 1))
            y += b[5] * jnp.where(first_digit, pltpu.roll(x, LANES - 31, 1), pltpu.roll(x, 1, 1))
            out.append(y)
        return v, out

    def spot(g, t):
        return pl.ds(pl.multiple_of(g * GROUP + t * LANES, LANES), LANES)

    load.wait()

    @pl.loop(0, outer, unroll=2)
    def _(g):
        us, ws = [], []
        for r in range(rows):
            v, y = apply_d(u, r, g)
            us.append(v)
            ws.append(y)
            for t in range(tiles):
                w[r, :, spot(g, t)] = y[t]
        for t in range(tiles):
            mine[0, :, spot(g, t)] = 2.0 * b[0] * ws[rows - 1][t] + b[0] * b[0] * us[rows - 2][t]
            mine[1, :, spot(g, t)] = 2.0 * a[0] * ws[0][t] + a[0] * a[0] * us[1][t]

    coarse_lane = (lane < 32) & (lane % 8 == 0)

    def pack(ref, r):
        halves = []
        for half in range(2):
            total = None
            for block in range(4):
                part = None
                for k in range(8):
                    i = half * 32 + block * 8 + k
                    start = (i // 16 * n3 + i // 4 % 4 * 2) * GROUP + i % 4 * LANES
                    x = jnp.where(coarse_lane, ref[r, :, start : start + LANES], 0.0)
                    x = x if k == 0 else pltpu.roll(x, k, 1)
                    part = x if part is None else part + x
                part = part if block == 0 else pltpu.roll(part, 32 * block, 1)
                total = part if total is None else total + part
            halves.append(total)
        return halves

    def store_pack(dst, slot, place, ref, r):
        low, high = pack(ref, r)
        dst[slot, place, :, 0:LANES] = low
        dst[slot, place, :, LANES : 2 * LANES] = high

    store_pack(c_out, 0, 0, u, rows - 1)
    store_pack(c_out, 0, 1, mine, 0)
    store_pack(c_out, 1, 0, u, 0)
    store_pack(c_out, 1, 1, mine, 1)

    coarse, bulk = [], []
    for s in range(2):
        coarse.append(
            pltpu.make_async_remote_copy(
                src_ref=c_out.at[s], dst_ref=c_in.at[s],
                send_sem=cs.at[s], recv_sem=cr.at[s],
                device_id=targets[s], device_id_type=MESH,
            )
        )
        coarse[-1].start()
    width = cells // chunks
    for c in range(chunks):
        for s in range(2):
            cut = (s, slice(None), pl.ds(c * width, width))
            bulk.append(
                pltpu.make_async_remote_copy(
                    src_ref=mine.at[cut], dst_ref=far.at[cut],
                    send_sem=far_s.at[s, c], recv_sem=far_r.at[s, c],
                    device_id=targets[s], device_id_type=MESH,
                )
            )
            bulk[-1].start()

    @pl.loop(0, outer, unroll=2)
    def _(g):
        for r in range(rows):
            _, y = apply_d(w, r, g)
            for t in range(tiles):
                x = y[t] + 2.0 * a[0] * b[0] * u[r, :, spot(g, t)]
                if r + 1 < rows:
                    x += 2.0 * a[0] * w[r + 1, :, spot(g, t)]
                if r >= 1:
                    x += 2.0 * b[0] * w[r - 1, :, spot(g, t)]
                if r + 2 < rows:
                    x += a[0] * a[0] * u[r + 2, :, spot(g, t)]
                if r >= 2:
                    x += b[0] * b[0] * u[r - 2, :, spot(g, t)]
                acc[r, :, spot(g, t)] = x

    scale = []
    for p in range(4):
        value = jnp.int32(0)
        for j in range(4):
            value = value + jnp.where(level_ref[0, p] == LOW + j, SIDE ** (3 - j), 0)
        scale.append(value)

    def placement(flat):
        target = jnp.zeros_like(flat)
        for p in range(4):
            target = target + ((flat >> LOW * (3 - p)) & (SIDE - 1)) * scale[p]
        return target

    row_id = lax.broadcasted_iota(jnp.int32, (COARSE, COARSE), 0)
    col_id = lax.broadcasted_iota(jnp.int32, (COARSE, COARSE), 1)
    col_line = lax.broadcasted_iota(jnp.int32, (1, COARSE), 1)
    row_line = lax.broadcasted_iota(jnp.int32, (COARSE, LANES), 0)
    one = lambda hit: jnp.where(hit, 1.0, 0.0).astype(jnp.bfloat16)
    forward = one(row_id == placement(col_line))
    row_target = placement(row_line)
    backward = one(col_id == jnp.concatenate([row_target] * (COARSE // LANES), axis=1))
    load_table.wait()
    dot = functools.partial(jnp.dot, preferred_element_type=jnp.float32)
    forward = dot(table[:, 0:COARSE], forward).astype(jnp.bfloat16)
    backward = dot(backward, table[:, COARSE : 2 * COARSE]).astype(jnp.bfloat16)

    pieces = [jnp.concatenate(pack(acc, r), axis=1) for r in range(rows)]
    for s in range(2):
        coarse[s].wait_recv()
    pieces[0] += c_in[0, 1]
    pieces[1] += b[0] * b[0] * c_in[0, 0]
    pieces[rows - 1] += c_in[1, 1]
    pieces[rows - 2] += a[0] * a[0] * c_in[1, 0]
    points = jnp.concatenate(pieces, axis=0)
    weighted = weight_ref[0].astype(jnp.float32) * exact_dot(points, forward)
    g_out[...] = weighted
    shares = []
    for k, peer in enumerate(peers):
        shares.append(
            pltpu.make_async_remote_copy(
                src_ref=g_out, dst_ref=g_in.at[k],
                send_sem=gs.at[k], recv_sem=gr.at[k],
                device_id=(peer, di), device_id_type=MESH,
            )
        )
        shares[-1].start()
    combined = weighted
    for k in range(len(peers)):
        shares[k].wait_recv()
        combined = combined + g_in[k]
    change = exact_dot(combined, backward) - points

    place = lax.broadcasted_iota(jnp.int32, (rows * second, LANES), 1)
    place = (place >> 5) * 2 + ((place >> 2) & 1)
    left = []
    for g in range(SIDE * SIDE):
        half = g // 8
        x = jnp.where(place == g % 8, change[:, half * LANES : (half + 1) * LANES], 0.0)
        high = x.astype(jnp.bfloat16)
        mid = (x - high.astype(jnp.float32)).astype(jnp.bfloat16)
        left.append(jnp.concatenate([high, mid], axis=1))
    fine = dot(jnp.concatenate(left, axis=0), table[:, 2 * COARSE :])
    for g in range(SIDE * SIDE):
        z[g] = fine[g * rows * second : (g + 1) * rows * second]

    for s in range(2):
        raw[s].wait_recv()

    @pl.loop(0, outer // 2)
    def _(i):
        after = (i & ~(SIDE - 1)) | ((i + 1) & (SIDE - 1))
        for r in range(rows):
            for t in range(tiles):
                cut = (pl.ds(r * second, second), slice(t * LANES, (t + 1) * LANES))
                even = z[(i,) + cut]
                odd = 0.5 * (even + z[(after,) + cut])
                for h, x in ((0, even), (1, odd)):
                    if r == 1:
                        x += b[0] * b[0] * near[0, :, spot(2 * i + h, t)]
                    if r == rows - 2:
                        x += a[0] * a[0] * near[1, :, spot(2 * i + h, t)]
                    acc[r, :, spot(2 * i + h, t)] += x

    saves = []
    for c in range(chunks):
        for s in range(2):
            bulk[2 * c + s].wait_recv()

        @pl.loop(0, width // GROUP, unroll=2)
        def _(i):
            for t in range(tiles):
                here = spot(c * (width // GROUP) + i, t)
                acc[0, :, here] += far[0, :, here]
                acc[rows - 1, :, here] += far[1, :, here]

        cut = (slice(None), slice(None), pl.ds(c * width, width))
        saves.append(pltpu.make_async_copy(acc.at[cut], out_ref.at[(0,) + cut], out_sem.at[c]))
        saves[-1].start()
    for copy in raw + coarse + bulk + shares:
        copy.wait_send()
    for copy in saves:
        copy.wait()


def local(grids, doms, state_field, level_vectors, combine_weights, diffusion, courant):
    _, rows, second, cells = state_field.shape
    chunks = 4
    table = jnp.asarray(constant_table())
    f32 = jnp.float32
    dma = pltpu.SemaphoreType.DMA
    smem = pl.BlockSpec(memory_space=pltpu.SMEM)
    anywhere = pl.BlockSpec(memory_space=pl.ANY)
    others = max(grids - 1, 1)
    return pl.pallas_call(
        functools.partial(kernel, grids, doms, chunks),
        out_shape=jax.ShapeDtypeStruct(state_field.shape, f32),
        in_specs=[smem] * 4 + [anywhere] * 2,
        out_specs=anywhere,
        scratch_shapes=[
            pltpu.VMEM((rows, second, cells), f32),
            pltpu.VMEM((rows, second, cells), f32),
            pltpu.VMEM((rows, second, cells), f32),
            pltpu.VMEM((2, second, cells), f32),
            pltpu.VMEM((2, second, cells), f32),
            pltpu.VMEM((2, second, cells), f32),
            pltpu.VMEM(table.shape, jnp.bfloat16),
            pltpu.VMEM((2, 2, second, COARSE), f32),
            pltpu.VMEM((2, 2, second, COARSE), f32),
            pltpu.VMEM((rows * second, COARSE), f32),
            pltpu.VMEM((others, rows * second, COARSE), f32),
            pltpu.VMEM((SIDE * SIDE, rows * second, GROUP), f32),
            dma((2,)),
            dma((2,)),
            dma((2,)),
            dma((2, chunks)),
            dma((2, chunks)),
            dma((2,)),
            dma((2,)),
            dma((others,)),
            dma((others,)),
            dma((chunks,)),
        ],
        compiler_params=pltpu.CompilerParams(
            collective_id=0, has_side_effects=True, vmem_limit_bytes=62 * 2**20
        ),
    )(level_vectors, combine_weights, diffusion, courant, state_field, table)


def solution(mesh):
    placed = (P("grid", "dom", None, None), P("grid", None), P("grid"), P(), P())
    return jax.shard_map(
        functools.partial(local, mesh.shape["grid"], mesh.shape["dom"]),
        mesh=mesh,
        in_specs=placed,
        out_specs=P("grid", "dom", None, None),
        check_vma=False,
    )
```

```python
import functools

import jax
import jax.numpy as jnp
import numpy as np
from jax import lax
from jax.experimental import pallas as pl
from jax.experimental.pallas import tpu as pltpu
from jax.sharding import PartitionSpec as P

LOW = 2
SIDE = 2**LOW
COARSE = SIDE**4
LANES = 128
GROUP = 16 * SIDE * SIDE * 2
MESH = pl.DeviceIdType.MESH


def level_matrix(length, orientation):
    ladder = [2**e for e in range(length.bit_length() - 1)]
    total = np.eye(length)
    for h in ladder if orientation < 0 else ladder[::-1]:
        step = np.eye(length)
        for i in range(h, length, 2 * h):
            step[i, (i - h) % length] += 0.5 * orientation
            step[i, (i + h) % length] += 0.5 * orientation
        total = step @ total
    return total


def kron4(m):
    return np.kron(np.kron(np.kron(m, m), m), m)


def packed_order():
    p = np.arange(COARSE)
    tile = p // LANES * 32 + p % LANES // 32 * 8 + p % 8
    return tile * 4 + p % 32 // 8


def interpolation(ratio):
    fine = np.arange(ratio * SIDE)
    gap = (fine[None, :] - ratio * np.arange(SIDE)[:, None]) % (ratio * SIDE)
    reach = np.minimum(gap, ratio * SIDE - gap)
    return np.maximum(1.0 - reach / ratio, 0.0)


def constant_table():
    down = kron4(level_matrix(SIDE, -1.0)).T[packed_order()]
    up = kron4(level_matrix(SIDE, 1.0)).T[:, packed_order()]
    spread = np.kron(interpolation(4), interpolation(8))
    spread = spread[packed_order()[:LANES] % spread.shape[0]]
    spread = np.concatenate([spread, spread], axis=0)
    return np.concatenate([down, up, spread], axis=1).astype(jnp.bfloat16)


def parts_of(x):
    high = x.astype(jnp.bfloat16)
    rest = x - high.astype(jnp.float32)
    mid = rest.astype(jnp.bfloat16)
    low = (rest - mid.astype(jnp.float32)).astype(jnp.bfloat16)
    return high, mid, low


def exact_dot(x, table):
    n = x.shape[0]
    y = jnp.dot(jnp.concatenate(parts_of(x), axis=0), table, preferred_element_type=jnp.float32)
    return y[0:n] + (y[n : 2 * n] + y[2 * n : 3 * n])


def kernel(
    grids, doms, chunks,
    level_ref, weight_ref, diff_ref, cour_ref, state_ref, table_hbm,
    out_ref, far,
    u, w, acc, near, mine, table, c_out, c_in, g_out, g_in, z,
    in_sem, raw_s, raw_r, far_s, far_r, cs, cr, gs, gr, out_sem,
):
    rows, second, cells = u.shape
    gi, di = lax.axis_index("grid"), lax.axis_index("dom")
    above, below = lax.rem(di + 1, doms), lax.rem(di + doms - 1, doms)
    peers = [lax.rem(gi + k, grids) for k in range(1, grids)]

    barrier = pltpu.get_barrier_semaphore()
    for side in (above, below):
        pl.semaphore_signal(barrier, inc=1, device_id=(gi, side), device_id_type=MESH)
    for peer in peers:
        pl.semaphore_signal(barrier, inc=1, device_id=(peer, di), device_id_type=MESH)
    load = pltpu.make_async_copy(state_ref.at[0], u, in_sem.at[0])
    load.start()
    load_table = pltpu.make_async_copy(table_hbm, table, in_sem.at[1])
    load_table.start()
    pl.semaphore_wait(barrier, 2 + len(peers))

    targets = ((gi, above), (gi, below))
    raw = []
    for s, row in ((0, rows - 1), (1, 0)):
        raw.append(
            pltpu.make_async_remote_copy(
                src_ref=state_ref.at[0, row], dst_ref=near.at[s],
                send_sem=raw_s.at[s], recv_sem=raw_r.at[s],
                device_id=targets[s], device_id_type=MESH,
            )
        )
        raw[-1].start()

    kappa, sigma = [diff_ref[0], diff_ref[1]], [cour_ref[0], cour_ref[1]]
    for j in range(4):
        k_sum, s_sum = jnp.float32(0.0), jnp.float32(0.0)
        for p in range(4):
            here = level_ref[0, p] == LOW + j
            k_sum = k_sum + jnp.where(here, diff_ref[2 + p], 0.0)
            s_sum = s_sum + jnp.where(here, cour_ref[2 + p], 0.0)
        kappa.append(k_sum)
        sigma.append(s_sum)
    a = [k - 0.5 * s for k, s in zip(kappa, sigma)]
    b = [k + 0.5 * s for k, s in zip(kappa, sigma)]
    centre = 1.0 - 2.0 * (kappa[0] + kappa[1] + kappa[2] + kappa[3] + kappa[4] + kappa[5])

    lane = lax.broadcasted_iota(jnp.int32, (second, LANES), 1)
    digit = lane % 32
    first_digit, last_digit = digit == 0, digit == 31
    in_low, in_high = lane < LANES - 32, lane >= 32
    tiles = GROUP // LANES
    outer = cells // GROUP
    n3 = 2 * SIDE

    def neighbours(g):
        base, low = g & ~(n3 - 1), n3 - 1
        ids = [(g + n3) & (outer - 1), (g - n3) & (outer - 1)]
        ids += [base | ((g + 1) & low), base | ((g - 1) & low)]
        return [i * GROUP for i in ids]

    def apply_d(ref, r, g):
        here = g * GROUP
        n = neighbours(g)
        at = lambda start, t: ref[r, :, pl.ds(pl.multiple_of(start + t * LANES, LANES), LANES)]
        v = [at(here, t) for t in range(tiles)]
        ahead = [pltpu.roll(x, LANES - 32, 1) for x in v]
        behind = [pltpu.roll(x, 32, 1) for x in v]
        out = []
        for t, x in enumerate(v):
            y = centre * x
            y += a[1] * pltpu.roll(x, second - 1, 0) + b[1] * pltpu.roll(x, 1, 0)
            y += a[2] * at(n[0], t) + b[2] * at(n[1], t)
            y += a[3] * at(n[2], t) + b[3] * at(n[3], t)
            y += a[4] * jnp.where(in_low, ahead[t], ahead[(t + 1) % tiles])
            y += b[4] * jnp.where(in_high, behind[t], behind[(t - 1) % tiles])
            y += a[5] * jnp.where(last_digit, pltpu.roll(x, 31, 1), pltpu.roll(x, LANES - 1, 1))
            y += b[5] * jnp.where(first_digit, pltpu.roll(x, LANES - 31, 1), pltpu.roll(x, 1, 1))
            out.append(y)
        return v, out

    def spot(g, t):
        return pl.ds(pl.multiple_of(g * GROUP + t * LANES, LANES), LANES)

    load.wait()

    @pl.loop(0, outer, unroll=2)
    def _(g):
        us, ws = [], []
        for r in range(rows):
            v, y = apply_d(u, r, g)
            us.append(v)
            ws.append(y)
            for t in range(tiles):
                w[r, :, spot(g, t)] = y[t]
        for t in range(tiles):
            mine[0, :, spot(g, t)] = 2.0 * b[0] * ws[rows - 1][t] + b[0] * b[0] * us[rows - 2][t]
            mine[1, :, spot(g, t)] = 2.0 * a[0] * ws[0][t] + a[0] * a[0] * us[1][t]

    coarse_lane = (lane < 32) & (lane % 8 == 0)

    def pack(ref, r):
        halves = []
        for half in range(2):
            total = None
            for block in range(4):
                part = None
                for k in range(8):
                    i = half * 32 + block * 8 + k
                    start = (i // 16 * n3 + i // 4 % 4 * 2) * GROUP + i % 4 * LANES
                    x = jnp.where(coarse_lane, ref[r, :, start : start + LANES], 0.0)
                    x = x if k == 0 else pltpu.roll(x, k, 1)
                    part = x if part is None else part + x
                part = part if block == 0 else pltpu.roll(part, 32 * block, 1)
                total = part if total is None else total + part
            halves.append(total)
        return halves

    def store_pack(dst, slot, place, ref, r):
        low, high = pack(ref, r)
        dst[slot, place, :, 0:LANES] = low
        dst[slot, place, :, LANES : 2 * LANES] = high

    store_pack(c_out, 0, 0, u, rows - 1)
    store_pack(c_out, 0, 1, mine, 0)
    store_pack(c_out, 1, 0, u, 0)
    store_pack(c_out, 1, 1, mine, 1)

    coarse, bulk = [], []
    for s in range(2):
        coarse.append(
            pltpu.make_async_remote_copy(
                src_ref=c_out.at[s], dst_ref=c_in.at[s],
                send_sem=cs.at[s], recv_sem=cr.at[s],
                device_id=targets[s], device_id_type=MESH,
            )
        )
        coarse[-1].start()
    width = cells // chunks
    for c in range(chunks):
        for s in range(2):
            cut = (s, slice(None), pl.ds(c * width, width))
            bulk.append(
                pltpu.make_async_remote_copy(
                    src_ref=mine.at[cut], dst_ref=far.at[cut],
                    send_sem=far_s.at[s, c], recv_sem=far_r.at[s, c],
                    device_id=targets[s], device_id_type=MESH,
                )
            )
            bulk[-1].start()

    @pl.loop(0, outer, unroll=2)
    def _(g):
        for r in range(rows):
            _, y = apply_d(w, r, g)
            for t in range(tiles):
                x = y[t] + 2.0 * a[0] * b[0] * u[r, :, spot(g, t)]
                if r + 1 < rows:
                    x += 2.0 * a[0] * w[r + 1, :, spot(g, t)]
                if r >= 1:
                    x += 2.0 * b[0] * w[r - 1, :, spot(g, t)]
                if r + 2 < rows:
                    x += a[0] * a[0] * u[r + 2, :, spot(g, t)]
                if r >= 2:
                    x += b[0] * b[0] * u[r - 2, :, spot(g, t)]
                acc[r, :, spot(g, t)] = x

    scale = []
    for p in range(4):
        value = jnp.int32(0)
        for j in range(4):
            value = value + jnp.where(level_ref[0, p] == LOW + j, SIDE ** (3 - j), 0)
        scale.append(value)

    def placement(flat):
        target = jnp.zeros_like(flat)
        for p in range(4):
            target = target + ((flat >> LOW * (3 - p)) & (SIDE - 1)) * scale[p]
        return target

    row_id = lax.broadcasted_iota(jnp.int32, (COARSE, COARSE), 0)
    col_id = lax.broadcasted_iota(jnp.int32, (COARSE, COARSE), 1)
    col_line = lax.broadcasted_iota(jnp.int32, (1, COARSE), 1)
    row_line = lax.broadcasted_iota(jnp.int32, (COARSE, LANES), 0)
    one = lambda hit: jnp.where(hit, 1.0, 0.0).astype(jnp.bfloat16)
    forward = one(row_id == placement(col_line))
    row_target = placement(row_line)
    backward = one(col_id == jnp.concatenate([row_target] * (COARSE // LANES), axis=1))
    load_table.wait()
    dot = functools.partial(jnp.dot, preferred_element_type=jnp.float32)
    forward = dot(table[:, 0:COARSE], forward).astype(jnp.bfloat16)
    backward = dot(backward, table[:, COARSE : 2 * COARSE]).astype(jnp.bfloat16)

    pieces = [jnp.concatenate(pack(acc, r), axis=1) for r in range(rows)]
    for s in range(2):
        coarse[s].wait_recv()
    pieces[0] += c_in[0, 1]
    pieces[1] += b[0] * b[0] * c_in[0, 0]
    pieces[rows - 1] += c_in[1, 1]
    pieces[rows - 2] += a[0] * a[0] * c_in[1, 0]
    points = jnp.concatenate(pieces, axis=0)
    weighted = weight_ref[0].astype(jnp.float32) * exact_dot(points, forward)
    g_out[...] = weighted
    shares = []
    for k, peer in enumerate(peers):
        shares.append(
            pltpu.make_async_remote_copy(
                src_ref=g_out, dst_ref=g_in.at[k],
                send_sem=gs.at[k], recv_sem=gr.at[k],
                device_id=(peer, di), device_id_type=MESH,
            )
        )
        shares[-1].start()
    combined = weighted
    for k in range(len(peers)):
        shares[k].wait_recv()
        combined = combined + g_in[k]
    change = exact_dot(combined, backward) - points

    place = lax.broadcasted_iota(jnp.int32, (rows * second, LANES), 1)
    place = (place >> 5) * 2 + ((place >> 2) & 1)
    left = []
    for g in range(SIDE * SIDE):
        half = g // 8
        x = jnp.where(place == g % 8, change[:, half * LANES : (half + 1) * LANES], 0.0)
        high = x.astype(jnp.bfloat16)
        mid = (x - high.astype(jnp.float32)).astype(jnp.bfloat16)
        left.append(jnp.concatenate([high, mid], axis=1))
    fine = dot(jnp.concatenate(left, axis=0), table[:, 2 * COARSE :])
    for g in range(SIDE * SIDE):
        z[g] = fine[g * rows * second : (g + 1) * rows * second]

    for s in range(2):
        raw[s].wait_recv()

    @pl.loop(0, outer // 2)
    def _(i):
        after = (i & ~(SIDE - 1)) | ((i + 1) & (SIDE - 1))
        for r in range(rows):
            for t in range(tiles):
                cut = (pl.ds(r * second, second), slice(t * LANES, (t + 1) * LANES))
                even = z[(i,) + cut]
                odd = 0.5 * (even + z[(after,) + cut])
                for h, x in ((0, even), (1, odd)):
                    if r == 1:
                        x += b[0] * b[0] * near[0, :, spot(2 * i + h, t)]
                    if r == rows - 2:
                        x += a[0] * a[0] * near[1, :, spot(2 * i + h, t)]
                    acc[r, :, spot(2 * i + h, t)] += x

    save = pltpu.make_async_copy(acc, out_ref, out_sem.at[0])
    save.start()
    for copy in bulk:
        copy.wait_recv()
    for copy in raw + coarse + bulk + shares:
        copy.wait_send()
    save.wait()


def local(grids, doms, state_field, level_vectors, combine_weights, diffusion, courant):
    _, rows, second, cells = state_field.shape
    chunks = 4
    table = jnp.asarray(constant_table())
    f32 = jnp.float32
    dma = pltpu.SemaphoreType.DMA
    smem = pl.BlockSpec(memory_space=pltpu.SMEM)
    anywhere = pl.BlockSpec(memory_space=pl.ANY)
    others = max(grids - 1, 1)
    own, far = pl.pallas_call(
        functools.partial(kernel, grids, doms, chunks),
        out_shape=[
            jax.ShapeDtypeStruct((rows, second, cells), f32),
            jax.ShapeDtypeStruct((2, second, cells), f32),
        ],
        in_specs=[smem] * 4 + [pl.BlockSpec(memory_space=pltpu.HBM)] * 2,
        out_specs=[anywhere] * 2,
        scratch_shapes=[
            pltpu.VMEM((rows, second, cells), f32),
            pltpu.VMEM((rows, second, cells), f32),
            pltpu.VMEM((rows, second, cells), f32),
            pltpu.VMEM((2, second, cells), f32),
            pltpu.VMEM((2, second, cells), f32),
            pltpu.VMEM(table.shape, jnp.bfloat16),
            pltpu.VMEM((2, 2, second, COARSE), f32),
            pltpu.VMEM((2, 2, second, COARSE), f32),
            pltpu.VMEM((rows * second, COARSE), f32),
            pltpu.VMEM((others, rows * second, COARSE), f32),
            pltpu.VMEM((SIDE * SIDE, rows * second, GROUP), f32),
            dma((2,)),
            dma((2,)),
            dma((2,)),
            dma((2, chunks)),
            dma((2, chunks)),
            dma((2,)),
            dma((2,)),
            dma((others,)),
            dma((others,)),
            dma((1,)),
        ],
        compiler_params=pltpu.CompilerParams(
            collective_id=0, has_side_effects=True, vmem_limit_bytes=40 * 2**20
        ),
    )(level_vectors, combine_weights, diffusion, courant, state_field, table)
    if rows == 2:
        return (own + far)[None]
    parts = [own[:1] + far[:1], own[1:-1], own[-1:] + far[1:]]
    return jnp.concatenate(parts, axis=0)[None]


def solution(mesh):
    placed = (P("grid", "dom", None, None), P("grid", None), P("grid"), P(), P())
    return jax.shard_map(
        functools.partial(local, mesh.shape["grid"], mesh.shape["dom"]),
        mesh=mesh,
        in_specs=placed,
        out_specs=P("grid", "dom", None, None),
        check_vma=False,
    )
```

```python
import functools

import jax
import jax.numpy as jnp
import numpy as np
from jax import lax
from jax.experimental import pallas as pl
from jax.experimental.pallas import tpu as pltpu
from jax.sharding import PartitionSpec as P

LOW = 2
SIDE = 2**LOW
COARSE = SIDE**4
LANES = 128
GROUP = 16 * SIDE * SIDE * 2
MESH = pl.DeviceIdType.MESH


def level_matrix(length, orientation):
    ladder = [2**e for e in range(length.bit_length() - 1)]
    total = np.eye(length)
    for h in ladder if orientation < 0 else ladder[::-1]:
        step = np.eye(length)
        for i in range(h, length, 2 * h):
            step[i, (i - h) % length] += 0.5 * orientation
            step[i, (i + h) % length] += 0.5 * orientation
        total = step @ total
    return total


def kron4(m):
    return np.kron(np.kron(np.kron(m, m), m), m)


def packed_order():
    p = np.arange(COARSE)
    tile = p // LANES * 32 + p % LANES // 32 * 8 + p % 8
    return tile * 4 + p % 32 // 8


def interpolation(ratio):
    fine = np.arange(ratio * SIDE)
    gap = (fine[None, :] - ratio * np.arange(SIDE)[:, None]) % (ratio * SIDE)
    reach = np.minimum(gap, ratio * SIDE - gap)
    return np.maximum(1.0 - reach / ratio, 0.0)


def constant_table():
    down = kron4(level_matrix(SIDE, -1.0)).T[packed_order()]
    up = kron4(level_matrix(SIDE, 1.0)).T[:, packed_order()]
    spread = np.kron(interpolation(4), interpolation(8))
    spread = spread[packed_order()[:LANES] % spread.shape[0]]
    spread = np.concatenate([spread, spread], axis=0)
    return np.concatenate([down, up, spread], axis=1).astype(jnp.bfloat16)


def parts_of(x):
    high = x.astype(jnp.bfloat16)
    rest = x - high.astype(jnp.float32)
    mid = rest.astype(jnp.bfloat16)
    low = (rest - mid.astype(jnp.float32)).astype(jnp.bfloat16)
    return high, mid, low


def exact_dot(x, table):
    n = x.shape[0]
    y = jnp.dot(jnp.concatenate(parts_of(x), axis=0), table, preferred_element_type=jnp.float32)
    return y[0:n] + (y[n : 2 * n] + y[2 * n : 3 * n])


def kernel(
    grids, doms, chunks,
    level_ref, weight_ref, diff_ref, cour_ref, state_ref, table_hbm,
    out_ref, far,
    u, w, acc, near, mine, table, c_out, c_in, g_out, g_in, z,
    in_sem, raw_s, raw_r, far_s, far_r, cs, cr, gs, gr, out_sem,
):
    rows, second, cells = u.shape
    gi, di = lax.axis_index("grid"), lax.axis_index("dom")
    above, below = lax.rem(di + 1, doms), lax.rem(di + doms - 1, doms)
    peers = [lax.rem(gi + k, grids) for k in range(1, grids)]

    barrier = pltpu.get_barrier_semaphore()
    for side in (above, below):
        pl.semaphore_signal(barrier, inc=1, device_id=(gi, side), device_id_type=MESH)
    for peer in peers:
        pl.semaphore_signal(barrier, inc=1, device_id=(peer, di), device_id_type=MESH)
    load = pltpu.make_async_copy(state_ref.at[0], u, in_sem.at[0])
    load.start()
    load_table = pltpu.make_async_copy(table_hbm, table, in_sem.at[1])
    load_table.start()
    pl.semaphore_wait(barrier, 2 + len(peers))

    targets = ((gi, above), (gi, below))
    raw = []
    for s, row in ((0, rows - 1), (1, 0)):
        raw.append(
            pltpu.make_async_remote_copy(
                src_ref=state_ref.at[0, row], dst_ref=near.at[s],
                send_sem=raw_s.at[s], recv_sem=raw_r.at[s],
                device_id=targets[s], device_id_type=MESH,
            )
        )
        raw[-1].start()

    kappa, sigma = [diff_ref[0], diff_ref[1]], [cour_ref[0], cour_ref[1]]
    for j in range(4):
        k_sum, s_sum = jnp.float32(0.0), jnp.float32(0.0)
        for p in range(4):
            here = level_ref[0, p] == LOW + j
            k_sum = k_sum + jnp.where(here, diff_ref[2 + p], 0.0)
            s_sum = s_sum + jnp.where(here, cour_ref[2 + p], 0.0)
        kappa.append(k_sum)
        sigma.append(s_sum)
    a = [k - 0.5 * s for k, s in zip(kappa, sigma)]
    b = [k + 0.5 * s for k, s in zip(kappa, sigma)]
    centre = 1.0 - 2.0 * (kappa[0] + kappa[1] + kappa[2] + kappa[3] + kappa[4] + kappa[5])

    lane = lax.broadcasted_iota(jnp.int32, (second, LANES), 1)
    digit = lane % 32
    first_digit, last_digit = digit == 0, digit == 31
    in_low, in_high = lane < LANES - 32, lane >= 32
    tiles = GROUP // LANES
    outer = cells // GROUP
    n3 = 2 * SIDE

    def neighbours(g):
        base, low = g & ~(n3 - 1), n3 - 1
        ids = [(g + n3) & (outer - 1), (g - n3) & (outer - 1)]
        ids += [base | ((g + 1) & low), base | ((g - 1) & low)]
        return [i * GROUP for i in ids]

    def apply_d(ref, r, g):
        here = g * GROUP
        n = neighbours(g)
        at = lambda start, t: ref[r, :, pl.ds(pl.multiple_of(start + t * LANES, LANES), LANES)]
        v = [at(here, t) for t in range(tiles)]
        ahead = [pltpu.roll(x, LANES - 32, 1) for x in v]
        behind = [pltpu.roll(x, 32, 1) for x in v]
        out = []
        for t, x in enumerate(v):
            y = centre * x
            y += a[1] * pltpu.roll(x, second - 1, 0) + b[1] * pltpu.roll(x, 1, 0)
            y += a[2] * at(n[0], t) + b[2] * at(n[1], t)
            y += a[3] * at(n[2], t) + b[3] * at(n[3], t)
            y += a[4] * jnp.where(in_low, ahead[t], ahead[(t + 1) % tiles])
            y += b[4] * jnp.where(in_high, behind[t], behind[(t - 1) % tiles])
            y += a[5] * jnp.where(last_digit, pltpu.roll(x, 31, 1), pltpu.roll(x, LANES - 1, 1))
            y += b[5] * jnp.where(first_digit, pltpu.roll(x, LANES - 31, 1), pltpu.roll(x, 1, 1))
            out.append(y)
        return v, out

    def spot(g, t):
        return pl.ds(pl.multiple_of(g * GROUP + t * LANES, LANES), LANES)

    load.wait()

    @pl.loop(0, outer, unroll=2)
    def _(g):
        us, ws = [], []
        for r in range(rows):
            v, y = apply_d(u, r, g)
            us.append(v)
            ws.append(y)
            for t in range(tiles):
                w[r, :, spot(g, t)] = y[t]
        for t in range(tiles):
            mine[0, :, spot(g, t)] = 2.0 * b[0] * ws[rows - 1][t] + b[0] * b[0] * us[rows - 2][t]
            mine[1, :, spot(g, t)] = 2.0 * a[0] * ws[0][t] + a[0] * a[0] * us[1][t]

    coarse_lane = (lane < 32) & (lane % 8 == 0)

    def pack(ref, r):
        halves = []
        for half in range(2):
            total = None
            for block in range(4):
                part = None
                for k in range(8):
                    i = half * 32 + block * 8 + k
                    start = (i // 16 * n3 + i // 4 % 4 * 2) * GROUP + i % 4 * LANES
                    x = jnp.where(coarse_lane, ref[r, :, start : start + LANES], 0.0)
                    x = x if k == 0 else pltpu.roll(x, k, 1)
                    part = x if part is None else part + x
                part = part if block == 0 else pltpu.roll(part, 32 * block, 1)
                total = part if total is None else total + part
            halves.append(total)
        return halves

    def store_pack(dst, slot, place, ref, r):
        low, high = pack(ref, r)
        dst[slot, place, :, 0:LANES] = low
        dst[slot, place, :, LANES : 2 * LANES] = high

    store_pack(c_out, 0, 0, u, rows - 1)
    store_pack(c_out, 0, 1, mine, 0)
    store_pack(c_out, 1, 0, u, 0)
    store_pack(c_out, 1, 1, mine, 1)

    coarse, bulk = [], []
    for s in range(2):
        coarse.append(
            pltpu.make_async_remote_copy(
                src_ref=c_out.at[s], dst_ref=c_in.at[s],
                send_sem=cs.at[s], recv_sem=cr.at[s],
                device_id=targets[s], device_id_type=MESH,
            )
        )
        coarse[-1].start()
    width = cells // chunks
    for c in range(chunks):
        for s in range(2):
            cut = (s, slice(None), pl.ds(c * width, width))
            bulk.append(
                pltpu.make_async_remote_copy(
                    src_ref=mine.at[cut], dst_ref=far.at[cut],
                    send_sem=far_s.at[s, c], recv_sem=far_r.at[s, c],
                    device_id=targets[s], device_id_type=MESH,
                )
            )
            bulk[-1].start()

    @pl.loop(0, outer, unroll=2)
    def _(g):
        for r in range(rows):
            _, y = apply_d(w, r, g)
            for t in range(tiles):
                x = y[t] + 2.0 * a[0] * b[0] * u[r, :, spot(g, t)]
                if r + 1 < rows:
                    x += 2.0 * a[0] * w[r + 1, :, spot(g, t)]
                if r >= 1:
                    x += 2.0 * b[0] * w[r - 1, :, spot(g, t)]
                if r + 2 < rows:
                    x += a[0] * a[0] * u[r + 2, :, spot(g, t)]
                if r >= 2:
                    x += b[0] * b[0] * u[r - 2, :, spot(g, t)]
                acc[r, :, spot(g, t)] = x

    scale = []
    for p in range(4):
        value = jnp.int32(0)
        for j in range(4):
            value = value + jnp.where(level_ref[0, p] == LOW + j, SIDE ** (3 - j), 0)
        scale.append(value)

    def placement(flat):
        target = jnp.zeros_like(flat)
        for p in range(4):
            target = target + ((flat >> LOW * (3 - p)) & (SIDE - 1)) * scale[p]
        return target

    row_id = lax.broadcasted_iota(jnp.int32, (COARSE, COARSE), 0)
    col_id = lax.broadcasted_iota(jnp.int32, (COARSE, COARSE), 1)
    col_line = lax.broadcasted_iota(jnp.int32, (1, COARSE), 1)
    row_line = lax.broadcasted_iota(jnp.int32, (COARSE, LANES), 0)
    one = lambda hit: jnp.where(hit, 1.0, 0.0).astype(jnp.bfloat16)
    forward = one(row_id == placement(col_line))
    row_target = placement(row_line)
    backward = one(col_id == jnp.concatenate([row_target] * (COARSE // LANES), axis=1))
    load_table.wait()
    dot = functools.partial(jnp.dot, preferred_element_type=jnp.float32)
    forward = dot(table[:, 0:COARSE], forward).astype(jnp.bfloat16)
    backward = dot(backward, table[:, COARSE : 2 * COARSE]).astype(jnp.bfloat16)

    pieces = [jnp.concatenate(pack(acc, r), axis=1) for r in range(rows)]
    for s in range(2):
        coarse[s].wait_recv()
    pieces[0] += c_in[0, 1]
    pieces[1] += b[0] * b[0] * c_in[0, 0]
    pieces[rows - 1] += c_in[1, 1]
    pieces[rows - 2] += a[0] * a[0] * c_in[1, 0]
    points = jnp.concatenate(pieces, axis=0)
    weighted = weight_ref[0].astype(jnp.float32) * exact_dot(points, forward)
    g_out[...] = weighted
    shares = []
    for k, peer in enumerate(peers):
        shares.append(
            pltpu.make_async_remote_copy(
                src_ref=g_out, dst_ref=g_in.at[k],
                send_sem=gs.at[k], recv_sem=gr.at[k],
                device_id=(peer, di), device_id_type=MESH,
            )
        )
        shares[-1].start()
    combined = weighted
    for k in range(len(peers)):
        shares[k].wait_recv()
        combined = combined + g_in[k]
    change = exact_dot(combined, backward) - points

    place = lax.broadcasted_iota(jnp.int32, (rows * second, LANES), 1)
    place = (place >> 5) * 2 + ((place >> 2) & 1)
    left = []
    for g in range(SIDE * SIDE):
        half = g // 8
        x = jnp.where(place == g % 8, change[:, half * LANES : (half + 1) * LANES], 0.0)
        high = x.astype(jnp.bfloat16)
        mid = (x - high.astype(jnp.float32)).astype(jnp.bfloat16)
        left.append(jnp.concatenate([high, mid], axis=1))
    fine = dot(jnp.concatenate(left, axis=0), table[:, 2 * COARSE :])
    for g in range(SIDE * SIDE):
        z[g] = fine[g * rows * second : (g + 1) * rows * second]

    for s in range(2):
        raw[s].wait_recv()

    @pl.loop(0, outer // 2)
    def _(i):
        after = (i & ~(SIDE - 1)) | ((i + 1) & (SIDE - 1))
        for r in range(rows):
            for t in range(tiles):
                cut = (pl.ds(r * second, second), slice(t * LANES, (t + 1) * LANES))
                even = z[(i,) + cut]
                odd = 0.5 * (even + z[(after,) + cut])
                for h, x in ((0, even), (1, odd)):
                    if r == 1:
                        x += b[0] * b[0] * near[0, :, spot(2 * i + h, t)]
                    if r == rows - 2:
                        x += a[0] * a[0] * near[1, :, spot(2 * i + h, t)]
                    acc[r, :, spot(2 * i + h, t)] += x

    save = pltpu.make_async_copy(acc, out_ref, out_sem.at[0])
    save.start()
    for copy in bulk:
        copy.wait_recv()
    for copy in raw + coarse + bulk + shares:
        copy.wait_send()
    save.wait()


def local(grids, doms, state_field, level_vectors, combine_weights, diffusion, courant):
    _, rows, second, cells = state_field.shape
    chunks = 4
    table = jnp.asarray(constant_table())
    f32 = jnp.float32
    dma = pltpu.SemaphoreType.DMA
    smem = pl.BlockSpec(memory_space=pltpu.SMEM)
    anywhere = pl.BlockSpec(memory_space=pl.ANY)
    others = max(grids - 1, 1)
    own, far = pl.pallas_call(
        functools.partial(kernel, grids, doms, chunks),
        out_shape=[
            jax.ShapeDtypeStruct((rows, second, cells), f32),
            jax.ShapeDtypeStruct((2, second, cells), f32),
        ],
        in_specs=[smem] * 4 + [pl.BlockSpec(memory_space=pltpu.HBM)] * 2,
        out_specs=[anywhere] * 2,
        scratch_shapes=[
            pltpu.VMEM((rows, second, cells), f32),
            pltpu.VMEM((rows, second, cells), f32),
            pltpu.VMEM((rows, second, cells), f32),
            pltpu.VMEM((2, second, cells), f32),
            pltpu.VMEM((2, second, cells), f32),
            pltpu.VMEM(table.shape, jnp.bfloat16),
            pltpu.VMEM((2, 2, second, COARSE), f32),
            pltpu.VMEM((2, 2, second, COARSE), f32),
            pltpu.VMEM((rows * second, COARSE), f32),
            pltpu.VMEM((others, rows * second, COARSE), f32),
            pltpu.VMEM((SIDE * SIDE, rows * second, GROUP), f32),
            dma((2,)),
            dma((2,)),
            dma((2,)),
            dma((2, chunks)),
            dma((2, chunks)),
            dma((2,)),
            dma((2,)),
            dma((others,)),
            dma((others,)),
            dma((1,)),
        ],
        compiler_params=pltpu.CompilerParams(
            collective_id=0, has_side_effects=True, vmem_limit_bytes=62 * 2**20
        ),
    )(level_vectors, combine_weights, diffusion, courant, state_field, table)
    if rows == 2:
        return (own + far)[None]
    parts = [own[:1] + far[:1], own[1:-1], own[-1:] + far[1:]]
    return jnp.concatenate(parts, axis=0)[None]


def solution(mesh):
    placed = (P("grid", "dom", None, None), P("grid", None), P("grid"), P(), P())
    return jax.shard_map(
        functools.partial(local, mesh.shape["grid"], mesh.shape["dom"]),
        mesh=mesh,
        in_specs=placed,
        out_specs=P("grid", "dom", None, None),
        check_vma=False,
    )
```

```python
import functools

import jax
import jax.numpy as jnp
import numpy as np
from jax import lax
from jax.experimental import pallas as pl
from jax.experimental.pallas import tpu as pltpu
from jax.sharding import PartitionSpec as P

LOW = 2
SIDE = 2**LOW
COARSE = SIDE**4
LANES = 128
GROUP = 16 * SIDE * SIDE * 2
MESH = pl.DeviceIdType.MESH


def level_matrix(length, orientation):
    ladder = [2**e for e in range(length.bit_length() - 1)]
    total = np.eye(length)
    for h in ladder if orientation < 0 else ladder[::-1]:
        step = np.eye(length)
        for i in range(h, length, 2 * h):
            step[i, (i - h) % length] += 0.5 * orientation
            step[i, (i + h) % length] += 0.5 * orientation
        total = step @ total
    return total


def kron4(m):
    return np.kron(np.kron(np.kron(m, m), m), m)


def packed_order():
    p = np.arange(COARSE)
    tile = p // LANES * 32 + p % LANES // 32 * 8 + p % 8
    return tile * 4 + p % 32 // 8


def interpolation(ratio):
    fine = np.arange(ratio * SIDE)
    gap = (fine[None, :] - ratio * np.arange(SIDE)[:, None]) % (ratio * SIDE)
    reach = np.minimum(gap, ratio * SIDE - gap)
    return np.maximum(1.0 - reach / ratio, 0.0)


def constant_table():
    down = kron4(level_matrix(SIDE, -1.0)).T[packed_order()]
    up = kron4(level_matrix(SIDE, 1.0)).T[:, packed_order()]
    spread = np.kron(interpolation(4), interpolation(8))
    spread = spread[packed_order()[:LANES] % spread.shape[0]]
    spread = np.concatenate([spread, spread], axis=0)
    return np.concatenate([down, up, spread], axis=1).astype(jnp.bfloat16)


def parts_of(x):
    high = x.astype(jnp.bfloat16)
    rest = x - high.astype(jnp.float32)
    mid = rest.astype(jnp.bfloat16)
    low = (rest - mid.astype(jnp.float32)).astype(jnp.bfloat16)
    return high, mid, low


def exact_dot(x, table):
    n = x.shape[0]
    y = jnp.dot(jnp.concatenate(parts_of(x), axis=0), table, preferred_element_type=jnp.float32)
    return y[0:n] + (y[n : 2 * n] + y[2 * n : 3 * n])


def kernel(
    grids, doms, chunks,
    level_ref, weight_ref, diff_ref, cour_ref, state_ref, table_hbm,
    out_ref, far,
    u, w, acc, near, mine, table, c_out, c_in, g_out, g_in, z,
    in_sem, raw_s, raw_r, far_s, far_r, cs, cr, gs, gr, out_sem,
):
    rows, second, cells = u.shape
    gi, di = lax.axis_index("grid"), lax.axis_index("dom")
    above, below = lax.rem(di + 1, doms), lax.rem(di + doms - 1, doms)
    peers = [lax.rem(gi + k, grids) for k in range(1, grids)]

    barrier = pltpu.get_barrier_semaphore()
    for side in (above, below):
        pl.semaphore_signal(barrier, inc=1, device_id=(gi, side), device_id_type=MESH)
    for peer in peers:
        pl.semaphore_signal(barrier, inc=1, device_id=(peer, di), device_id_type=MESH)
    load = pltpu.make_async_copy(state_ref.at[0], u, in_sem.at[0])
    load.start()
    load_table = pltpu.make_async_copy(table_hbm, table, in_sem.at[1])
    load_table.start()
    pl.semaphore_wait(barrier, 2 + len(peers))

    targets = ((gi, above), (gi, below))
    raw = []
    for s, row in ((0, rows - 1), (1, 0)):
        raw.append(
            pltpu.make_async_remote_copy(
                src_ref=state_ref.at[0, row], dst_ref=near.at[s],
                send_sem=raw_s.at[s], recv_sem=raw_r.at[s],
                device_id=targets[s], device_id_type=MESH,
            )
        )
        raw[-1].start()

    kappa, sigma = [diff_ref[0], diff_ref[1]], [cour_ref[0], cour_ref[1]]
    for j in range(4):
        k_sum, s_sum = jnp.float32(0.0), jnp.float32(0.0)
        for p in range(4):
            here = level_ref[0, p] == LOW + j
            k_sum = k_sum + jnp.where(here, diff_ref[2 + p], 0.0)
            s_sum = s_sum + jnp.where(here, cour_ref[2 + p], 0.0)
        kappa.append(k_sum)
        sigma.append(s_sum)
    a = [k - 0.5 * s for k, s in zip(kappa, sigma)]
    b = [k + 0.5 * s for k, s in zip(kappa, sigma)]
    centre = 1.0 - 2.0 * (kappa[0] + kappa[1] + kappa[2] + kappa[3] + kappa[4] + kappa[5])

    lane = lax.broadcasted_iota(jnp.int32, (second, LANES), 1)
    digit = lane % 32
    first_digit, last_digit = digit == 0, digit == 31
    in_low, in_high = lane < LANES - 32, lane >= 32
    tiles = GROUP // LANES
    outer = cells // GROUP
    n3 = 2 * SIDE

    def neighbours(g):
        base, low = g & ~(n3 - 1), n3 - 1
        ids = [(g + n3) & (outer - 1), (g - n3) & (outer - 1)]
        ids += [base | ((g + 1) & low), base | ((g - 1) & low)]
        return [i * GROUP for i in ids]

    def apply_d(ref, r, g):
        here = g * GROUP
        n = neighbours(g)
        at = lambda start, t: ref[r, :, pl.ds(pl.multiple_of(start + t * LANES, LANES), LANES)]
        v = [at(here, t) for t in range(tiles)]
        ahead = [pltpu.roll(x, LANES - 32, 1) for x in v]
        behind = [pltpu.roll(x, 32, 1) for x in v]
        out = []
        for t, x in enumerate(v):
            y = centre * x
            y += a[1] * pltpu.roll(x, second - 1, 0) + b[1] * pltpu.roll(x, 1, 0)
            y += a[2] * at(n[0], t) + b[2] * at(n[1], t)
            y += a[3] * at(n[2], t) + b[3] * at(n[3], t)
            y += a[4] * jnp.where(in_low, ahead[t], ahead[(t + 1) % tiles])
            y += b[4] * jnp.where(in_high, behind[t], behind[(t - 1) % tiles])
            y += a[5] * jnp.where(last_digit, pltpu.roll(x, 31, 1), pltpu.roll(x, LANES - 1, 1))
            y += b[5] * jnp.where(first_digit, pltpu.roll(x, LANES - 31, 1), pltpu.roll(x, 1, 1))
            out.append(y)
        return v, out

    def spot(g, t):
        return pl.ds(pl.multiple_of(g * GROUP + t * LANES, LANES), LANES)

    load.wait()

    @pl.loop(0, outer, unroll=2)
    def _(g):
        us, ws = [], []
        for r in range(rows):
            v, y = apply_d(u, r, g)
            us.append(v)
            ws.append(y)
            for t in range(tiles):
                w[r, :, spot(g, t)] = y[t]
        for t in range(tiles):
            mine[0, :, spot(g, t)] = 2.0 * b[0] * ws[rows - 1][t] + b[0] * b[0] * us[rows - 2][t]
            mine[1, :, spot(g, t)] = 2.0 * a[0] * ws[0][t] + a[0] * a[0] * us[1][t]

    coarse_lane = (lane < 32) & (lane % 8 == 0)

    def pack(ref, r):
        halves = []
        for half in range(2):
            total = None
            for block in range(4):
                part = None
                for k in range(8):
                    i = half * 32 + block * 8 + k
                    start = (i // 16 * n3 + i // 4 % 4 * 2) * GROUP + i % 4 * LANES
                    x = jnp.where(coarse_lane, ref[r, :, start : start + LANES], 0.0)
                    x = x if k == 0 else pltpu.roll(x, k, 1)
                    part = x if part is None else part + x
                part = part if block == 0 else pltpu.roll(part, 32 * block, 1)
                total = part if total is None else total + part
            halves.append(total)
        return halves

    def store_pack(dst, slot, place, ref, r):
        low, high = pack(ref, r)
        dst[slot, place, :, 0:LANES] = low
        dst[slot, place, :, LANES : 2 * LANES] = high

    store_pack(c_out, 0, 0, u, rows - 1)
    store_pack(c_out, 0, 1, mine, 0)
    store_pack(c_out, 1, 0, u, 0)
    store_pack(c_out, 1, 1, mine, 1)

    coarse, bulk = [], []
    for s in range(2):
        coarse.append(
            pltpu.make_async_remote_copy(
                src_ref=c_out.at[s], dst_ref=c_in.at[s],
                send_sem=cs.at[s], recv_sem=cr.at[s],
                device_id=targets[s], device_id_type=MESH,
            )
        )
        coarse[-1].start()
    width = cells // chunks
    for c in range(chunks):
        for s in range(2):
            cut = (s, slice(None), pl.ds(c * width, width))
            bulk.append(
                pltpu.make_async_remote_copy(
                    src_ref=mine.at[cut], dst_ref=far.at[cut],
                    send_sem=far_s.at[s, c], recv_sem=far_r.at[s, c],
                    device_id=targets[s], device_id_type=MESH,
                )
            )
            bulk[-1].start()

    @pl.loop(0, outer, unroll=2)
    def _(g):
        for r in range(rows):
            _, y = apply_d(w, r, g)
            for t in range(tiles):
                x = y[t] + 2.0 * a[0] * b[0] * u[r, :, spot(g, t)]
                if r + 1 < rows:
                    x += 2.0 * a[0] * w[r + 1, :, spot(g, t)]
                if r >= 1:
                    x += 2.0 * b[0] * w[r - 1, :, spot(g, t)]
                if r + 2 < rows:
                    x += a[0] * a[0] * u[r + 2, :, spot(g, t)]
                if r >= 2:
                    x += b[0] * b[0] * u[r - 2, :, spot(g, t)]
                acc[r, :, spot(g, t)] = x

    scale = []
    for p in range(4):
        value = jnp.int32(0)
        for j in range(4):
            value = value + jnp.where(level_ref[0, p] == LOW + j, SIDE ** (3 - j), 0)
        scale.append(value)

    def placement(flat):
        target = jnp.zeros_like(flat)
        for p in range(4):
            target = target + ((flat >> LOW * (3 - p)) & (SIDE - 1)) * scale[p]
        return target

    row_id = lax.broadcasted_iota(jnp.int32, (COARSE, COARSE), 0)
    col_id = lax.broadcasted_iota(jnp.int32, (COARSE, COARSE), 1)
    col_line = lax.broadcasted_iota(jnp.int32, (1, COARSE), 1)
    row_line = lax.broadcasted_iota(jnp.int32, (COARSE, LANES), 0)
    one = lambda hit: jnp.where(hit, 1.0, 0.0).astype(jnp.bfloat16)
    forward = one(row_id == placement(col_line))
    row_target = placement(row_line)
    backward = one(col_id == jnp.concatenate([row_target] * (COARSE // LANES), axis=1))
    load_table.wait()
    dot = functools.partial(jnp.dot, preferred_element_type=jnp.float32)
    forward = dot(table[:, 0:COARSE], forward).astype(jnp.bfloat16)
    backward = dot(backward, table[:, COARSE : 2 * COARSE]).astype(jnp.bfloat16)

    pieces = [jnp.concatenate(pack(acc, r), axis=1) for r in range(rows)]
    for s in range(2):
        coarse[s].wait_recv()
    pieces[0] += c_in[0, 1]
    pieces[1] += b[0] * b[0] * c_in[0, 0]
    pieces[rows - 1] += c_in[1, 1]
    pieces[rows - 2] += a[0] * a[0] * c_in[1, 0]
    points = jnp.concatenate(pieces, axis=0)
    weighted = weight_ref[0].astype(jnp.float32) * exact_dot(points, forward)
    g_out[...] = weighted
    shares = []
    for k, peer in enumerate(peers):
        shares.append(
            pltpu.make_async_remote_copy(
                src_ref=g_out, dst_ref=g_in.at[k],
                send_sem=gs.at[k], recv_sem=gr.at[k],
                device_id=(peer, di), device_id_type=MESH,
            )
        )
        shares[-1].start()
    combined = weighted
    for k in range(len(peers)):
        shares[k].wait_recv()
        combined = combined + g_in[k]
    change = exact_dot(combined, backward) - points

    place = lax.broadcasted_iota(jnp.int32, (rows * second, LANES), 1)
    place = (place >> 5) * 2 + ((place >> 2) & 1)
    left = []
    for g in range(SIDE * SIDE):
        half = g // 8
        x = jnp.where(place == g % 8, change[:, half * LANES : (half + 1) * LANES], 0.0)
        high = x.astype(jnp.bfloat16)
        mid = (x - high.astype(jnp.float32)).astype(jnp.bfloat16)
        left.append(jnp.concatenate([high, mid], axis=1))
    fine = dot(jnp.concatenate(left, axis=0), table[:, 2 * COARSE :])
    for g in range(SIDE * SIDE):
        z[g] = fine[g * rows * second : (g + 1) * rows * second]

    for s in range(2):
        raw[s].wait_recv()

    @pl.loop(0, outer // 2)
    def _(i):
        after = (i & ~(SIDE - 1)) | ((i + 1) & (SIDE - 1))
        for r in range(rows):
            for t in range(tiles):
                cut = (pl.ds(r * second, second), slice(t * LANES, (t + 1) * LANES))
                even = z[(i,) + cut]
                odd = 0.5 * (even + z[(after,) + cut])
                for h, x in ((0, even), (1, odd)):
                    if r == 1:
                        x += b[0] * b[0] * near[0, :, spot(2 * i + h, t)]
                    if r == rows - 2:
                        x += a[0] * a[0] * near[1, :, spot(2 * i + h, t)]
                    acc[r, :, spot(2 * i + h, t)] += x

    save = pltpu.make_async_copy(acc, out_ref, out_sem.at[0])
    save.start()
    for copy in bulk:
        copy.wait_recv()
    for copy in raw + coarse + bulk + shares:
        copy.wait_send()
    save.wait()


def local(grids, doms, state_field, level_vectors, combine_weights, diffusion, courant):
    _, rows, second, cells = state_field.shape
    chunks = 4
    table = pltpu.with_memory_space_constraint(jnp.asarray(constant_table()), pltpu.HBM)
    state_in = pltpu.with_memory_space_constraint(state_field, pltpu.HBM)
    f32 = jnp.float32
    dma = pltpu.SemaphoreType.DMA
    smem = pl.BlockSpec(memory_space=pltpu.SMEM)
    anywhere = pl.BlockSpec(memory_space=pl.ANY)
    others = max(grids - 1, 1)
    own, far = pl.pallas_call(
        functools.partial(kernel, grids, doms, chunks),
        out_shape=[
            jax.ShapeDtypeStruct((rows, second, cells), f32),
            jax.ShapeDtypeStruct((2, second, cells), f32),
        ],
        in_specs=[smem] * 4 + [pl.BlockSpec(memory_space=pltpu.HBM)] * 2,
        out_specs=[anywhere] * 2,
        scratch_shapes=[
            pltpu.VMEM((rows, second, cells), f32),
            pltpu.VMEM((rows, second, cells), f32),
            pltpu.VMEM((rows, second, cells), f32),
            pltpu.VMEM((2, second, cells), f32),
            pltpu.VMEM((2, second, cells), f32),
            pltpu.VMEM(table.shape, jnp.bfloat16),
            pltpu.VMEM((2, 2, second, COARSE), f32),
            pltpu.VMEM((2, 2, second, COARSE), f32),
            pltpu.VMEM((rows * second, COARSE), f32),
            pltpu.VMEM((others, rows * second, COARSE), f32),
            pltpu.VMEM((SIDE * SIDE, rows * second, GROUP), f32),
            dma((2,)),
            dma((2,)),
            dma((2,)),
            dma((2, chunks)),
            dma((2, chunks)),
            dma((2,)),
            dma((2,)),
            dma((others,)),
            dma((others,)),
            dma((1,)),
        ],
        compiler_params=pltpu.CompilerParams(
            collective_id=0, has_side_effects=True, vmem_limit_bytes=40 * 2**20
        ),
    )(level_vectors, combine_weights, diffusion, courant, state_in, table)
    if rows == 2:
        return (own + far)[None]
    parts = [own[:1] + far[:1], own[1:-1], own[-1:] + far[1:]]
    return jnp.concatenate(parts, axis=0)[None]


def solution(mesh):
    placed = (P("grid", "dom", None, None), P("grid", None), P("grid"), P(), P())
    return jax.shard_map(
        functools.partial(local, mesh.shape["grid"], mesh.shape["dom"]),
        mesh=mesh,
        in_specs=placed,
        out_specs=P("grid", "dom", None, None),
        check_vma=False,
    )
```

```python
import functools

import jax
import jax.numpy as jnp
import numpy as np
from jax import lax
from jax.experimental import pallas as pl
from jax.experimental.pallas import tpu as pltpu
from jax.sharding import PartitionSpec as P

LOW = 2
SIDE = 2**LOW
COARSE = SIDE**4
LANES = 128
GROUP = 16 * SIDE * SIDE * 2
MESH = pl.DeviceIdType.MESH


def level_matrix(length, orientation):
    ladder = [2**e for e in range(length.bit_length() - 1)]
    total = np.eye(length)
    for h in ladder if orientation < 0 else ladder[::-1]:
        step = np.eye(length)
        for i in range(h, length, 2 * h):
            step[i, (i - h) % length] += 0.5 * orientation
            step[i, (i + h) % length] += 0.5 * orientation
        total = step @ total
    return total


def kron4(m):
    return np.kron(np.kron(np.kron(m, m), m), m)


def packed_order():
    p = np.arange(COARSE)
    tile = p // LANES * 32 + p % LANES // 32 * 8 + p % 8
    return tile * 4 + p % 32 // 8


def interpolation(ratio):
    fine = np.arange(ratio * SIDE)
    gap = (fine[None, :] - ratio * np.arange(SIDE)[:, None]) % (ratio * SIDE)
    reach = np.minimum(gap, ratio * SIDE - gap)
    return np.maximum(1.0 - reach / ratio, 0.0)


def constant_table():
    down = kron4(level_matrix(SIDE, -1.0)).T[packed_order()]
    up = kron4(level_matrix(SIDE, 1.0)).T[:, packed_order()]
    spread = np.kron(interpolation(4), interpolation(8))
    spread = spread[packed_order()[:LANES] % spread.shape[0]]
    spread = np.concatenate([spread, spread], axis=0)
    return np.concatenate([down, up, spread], axis=1).astype(jnp.bfloat16)


def parts_of(x):
    high = x.astype(jnp.bfloat16)
    rest = x - high.astype(jnp.float32)
    mid = rest.astype(jnp.bfloat16)
    low = (rest - mid.astype(jnp.float32)).astype(jnp.bfloat16)
    return high, mid, low


def exact_dot(x, table):
    n = x.shape[0]
    y = jnp.dot(jnp.concatenate(parts_of(x), axis=0), table, preferred_element_type=jnp.float32)
    return y[0:n] + (y[n : 2 * n] + y[2 * n : 3 * n])


def kernel(
    grids, doms, chunks,
    weight_ref, level_hbm, diff_hbm, cour_hbm, state_ref, table_hbm,
    out_ref, far,
    u, w, acc, near, mine, table, c_out, c_in, g_out, g_in, z,
    level_ref, diff_ref, cour_ref,
    in_sem, raw_s, raw_r, far_s, far_r, cs, cr, gs, gr, out_sem,
):
    rows, second, cells = u.shape
    gi, di = lax.axis_index("grid"), lax.axis_index("dom")
    above, below = lax.rem(di + 1, doms), lax.rem(di + doms - 1, doms)
    peers = [lax.rem(gi + k, grids) for k in range(1, grids)]

    barrier = pltpu.get_barrier_semaphore()
    for side in (above, below):
        pl.semaphore_signal(barrier, inc=1, device_id=(gi, side), device_id_type=MESH)
    for peer in peers:
        pl.semaphore_signal(barrier, inc=1, device_id=(peer, di), device_id_type=MESH)
    load = pltpu.make_async_copy(state_ref.at[0], u, in_sem.at[0])
    load.start()
    load_table = pltpu.make_async_copy(table_hbm, table, in_sem.at[1])
    load_table.start()
    smalls = []
    for k, (src, dst) in enumerate(
        (
            (level_hbm, level_ref),
            (diff_hbm, diff_ref),
            (cour_hbm, cour_ref),
        )
    ):
        smalls.append(pltpu.make_async_copy(src, dst, in_sem.at[2 + k]))
        smalls[-1].start()
    pl.semaphore_wait(barrier, 2 + len(peers))

    targets = ((gi, above), (gi, below))
    raw = []
    for s, row in ((0, rows - 1), (1, 0)):
        raw.append(
            pltpu.make_async_remote_copy(
                src_ref=state_ref.at[0, row], dst_ref=near.at[s],
                send_sem=raw_s.at[s], recv_sem=raw_r.at[s],
                device_id=targets[s], device_id_type=MESH,
            )
        )
        raw[-1].start()

    for copy in smalls:
        copy.wait()
    kappa, sigma = [diff_ref[0], diff_ref[1]], [cour_ref[0], cour_ref[1]]
    for j in range(4):
        k_sum, s_sum = jnp.float32(0.0), jnp.float32(0.0)
        for p in range(4):
            here = level_ref[0, p] == LOW + j
            k_sum = k_sum + jnp.where(here, diff_ref[2 + p], 0.0)
            s_sum = s_sum + jnp.where(here, cour_ref[2 + p], 0.0)
        kappa.append(k_sum)
        sigma.append(s_sum)
    a = [k - 0.5 * s for k, s in zip(kappa, sigma)]
    b = [k + 0.5 * s for k, s in zip(kappa, sigma)]
    centre = 1.0 - 2.0 * (kappa[0] + kappa[1] + kappa[2] + kappa[3] + kappa[4] + kappa[5])

    lane = lax.broadcasted_iota(jnp.int32, (second, LANES), 1)
    digit = lane % 32
    first_digit, last_digit = digit == 0, digit == 31
    in_low, in_high = lane < LANES - 32, lane >= 32
    tiles = GROUP // LANES
    outer = cells // GROUP
    n3 = 2 * SIDE

    def neighbours(g):
        base, low = g & ~(n3 - 1), n3 - 1
        ids = [(g + n3) & (outer - 1), (g - n3) & (outer - 1)]
        ids += [base | ((g + 1) & low), base | ((g - 1) & low)]
        return [i * GROUP for i in ids]

    def apply_d(ref, r, g):
        here = g * GROUP
        n = neighbours(g)
        at = lambda start, t: ref[r, :, pl.ds(pl.multiple_of(start + t * LANES, LANES), LANES)]
        v = [at(here, t) for t in range(tiles)]
        ahead = [pltpu.roll(x, LANES - 32, 1) for x in v]
        behind = [pltpu.roll(x, 32, 1) for x in v]
        out = []
        for t, x in enumerate(v):
            y = centre * x
            y += a[1] * pltpu.roll(x, second - 1, 0) + b[1] * pltpu.roll(x, 1, 0)
            y += a[2] * at(n[0], t) + b[2] * at(n[1], t)
            y += a[3] * at(n[2], t) + b[3] * at(n[3], t)
            y += a[4] * jnp.where(in_low, ahead[t], ahead[(t + 1) % tiles])
            y += b[4] * jnp.where(in_high, behind[t], behind[(t - 1) % tiles])
            y += a[5] * jnp.where(last_digit, pltpu.roll(x, 31, 1), pltpu.roll(x, LANES - 1, 1))
            y += b[5] * jnp.where(first_digit, pltpu.roll(x, LANES - 31, 1), pltpu.roll(x, 1, 1))
            out.append(y)
        return v, out

    def spot(g, t):
        return pl.ds(pl.multiple_of(g * GROUP + t * LANES, LANES), LANES)

    load.wait()

    @pl.loop(0, outer, unroll=2)
    def _(g):
        us, ws = [], []
        for r in range(rows):
            v, y = apply_d(u, r, g)
            us.append(v)
            ws.append(y)
            for t in range(tiles):
                w[r, :, spot(g, t)] = y[t]
        for t in range(tiles):
            mine[0, :, spot(g, t)] = 2.0 * b[0] * ws[rows - 1][t] + b[0] * b[0] * us[rows - 2][t]
            mine[1, :, spot(g, t)] = 2.0 * a[0] * ws[0][t] + a[0] * a[0] * us[1][t]

    coarse_lane = (lane < 32) & (lane % 8 == 0)

    def pack(ref, r):
        halves = []
        for half in range(2):
            total = None
            for block in range(4):
                part = None
                for k in range(8):
                    i = half * 32 + block * 8 + k
                    start = (i // 16 * n3 + i // 4 % 4 * 2) * GROUP + i % 4 * LANES
                    x = jnp.where(coarse_lane, ref[r, :, start : start + LANES], 0.0)
                    x = x if k == 0 else pltpu.roll(x, k, 1)
                    part = x if part is None else part + x
                part = part if block == 0 else pltpu.roll(part, 32 * block, 1)
                total = part if total is None else total + part
            halves.append(total)
        return halves

    def store_pack(dst, slot, place, ref, r):
        low, high = pack(ref, r)
        dst[slot, place, :, 0:LANES] = low
        dst[slot, place, :, LANES : 2 * LANES] = high

    store_pack(c_out, 0, 0, u, rows - 1)
    store_pack(c_out, 0, 1, mine, 0)
    store_pack(c_out, 1, 0, u, 0)
    store_pack(c_out, 1, 1, mine, 1)

    coarse, bulk = [], []
    for s in range(2):
        coarse.append(
            pltpu.make_async_remote_copy(
                src_ref=c_out.at[s], dst_ref=c_in.at[s],
                send_sem=cs.at[s], recv_sem=cr.at[s],
                device_id=targets[s], device_id_type=MESH,
            )
        )
        coarse[-1].start()
    width = cells // chunks
    for c in range(chunks):
        for s in range(2):
            cut = (s, slice(None), pl.ds(c * width, width))
            bulk.append(
                pltpu.make_async_remote_copy(
                    src_ref=mine.at[cut], dst_ref=far.at[cut],
                    send_sem=far_s.at[s, c], recv_sem=far_r.at[s, c],
                    device_id=targets[s], device_id_type=MESH,
                )
            )
            bulk[-1].start()

    @pl.loop(0, outer, unroll=2)
    def _(g):
        for r in range(rows):
            _, y = apply_d(w, r, g)
            for t in range(tiles):
                x = y[t] + 2.0 * a[0] * b[0] * u[r, :, spot(g, t)]
                if r + 1 < rows:
                    x += 2.0 * a[0] * w[r + 1, :, spot(g, t)]
                if r >= 1:
                    x += 2.0 * b[0] * w[r - 1, :, spot(g, t)]
                if r + 2 < rows:
                    x += a[0] * a[0] * u[r + 2, :, spot(g, t)]
                if r >= 2:
                    x += b[0] * b[0] * u[r - 2, :, spot(g, t)]
                acc[r, :, spot(g, t)] = x

    scale = []
    for p in range(4):
        value = jnp.int32(0)
        for j in range(4):
            value = value + jnp.where(level_ref[0, p] == LOW + j, SIDE ** (3 - j), 0)
        scale.append(value)

    def placement(flat):
        target = jnp.zeros_like(flat)
        for p in range(4):
            target = target + ((flat >> LOW * (3 - p)) & (SIDE - 1)) * scale[p]
        return target

    row_id = lax.broadcasted_iota(jnp.int32, (COARSE, COARSE), 0)
    col_id = lax.broadcasted_iota(jnp.int32, (COARSE, COARSE), 1)
    col_line = lax.broadcasted_iota(jnp.int32, (1, COARSE), 1)
    row_line = lax.broadcasted_iota(jnp.int32, (COARSE, LANES), 0)
    one = lambda hit: jnp.where(hit, 1.0, 0.0).astype(jnp.bfloat16)
    forward = one(row_id == placement(col_line))
    row_target = placement(row_line)
    backward = one(col_id == jnp.concatenate([row_target] * (COARSE // LANES), axis=1))
    load_table.wait()
    dot = functools.partial(jnp.dot, preferred_element_type=jnp.float32)
    forward = dot(table[:, 0:COARSE], forward).astype(jnp.bfloat16)
    backward = dot(backward, table[:, COARSE : 2 * COARSE]).astype(jnp.bfloat16)

    pieces = [jnp.concatenate(pack(acc, r), axis=1) for r in range(rows)]
    for s in range(2):
        coarse[s].wait_recv()
    pieces[0] += c_in[0, 1]
    pieces[1] += b[0] * b[0] * c_in[0, 0]
    pieces[rows - 1] += c_in[1, 1]
    pieces[rows - 2] += a[0] * a[0] * c_in[1, 0]
    points = jnp.concatenate(pieces, axis=0)
    weighted = weight_ref[0].astype(jnp.float32) * exact_dot(points, forward)
    g_out[...] = weighted
    shares = []
    for k, peer in enumerate(peers):
        shares.append(
            pltpu.make_async_remote_copy(
                src_ref=g_out, dst_ref=g_in.at[k],
                send_sem=gs.at[k], recv_sem=gr.at[k],
                device_id=(peer, di), device_id_type=MESH,
            )
        )
        shares[-1].start()
    combined = weighted
    for k in range(len(peers)):
        shares[k].wait_recv()
        combined = combined + g_in[k]
    change = exact_dot(combined, backward) - points

    place = lax.broadcasted_iota(jnp.int32, (rows * second, LANES), 1)
    place = (place >> 5) * 2 + ((place >> 2) & 1)
    left = []
    for g in range(SIDE * SIDE):
        half = g // 8
        x = jnp.where(place == g % 8, change[:, half * LANES : (half + 1) * LANES], 0.0)
        high = x.astype(jnp.bfloat16)
        mid = (x - high.astype(jnp.float32)).astype(jnp.bfloat16)
        left.append(jnp.concatenate([high, mid], axis=1))
    fine = dot(jnp.concatenate(left, axis=0), table[:, 2 * COARSE :])
    for g in range(SIDE * SIDE):
        z[g] = fine[g * rows * second : (g + 1) * rows * second]

    for s in range(2):
        raw[s].wait_recv()

    @pl.loop(0, outer // 2)
    def _(i):
        after = (i & ~(SIDE - 1)) | ((i + 1) & (SIDE - 1))
        for r in range(rows):
            for t in range(tiles):
                cut = (pl.ds(r * second, second), slice(t * LANES, (t + 1) * LANES))
                even = z[(i,) + cut]
                odd = 0.5 * (even + z[(after,) + cut])
                for h, x in ((0, even), (1, odd)):
                    if r == 1:
                        x += b[0] * b[0] * near[0, :, spot(2 * i + h, t)]
                    if r == rows - 2:
                        x += a[0] * a[0] * near[1, :, spot(2 * i + h, t)]
                    acc[r, :, spot(2 * i + h, t)] += x

    save = pltpu.make_async_copy(acc, out_ref, out_sem.at[0])
    save.start()
    for copy in bulk:
        copy.wait_recv()
    for copy in raw + coarse + bulk + shares:
        copy.wait_send()
    save.wait()


def local(grids, doms, state_field, level_vectors, combine_weights, diffusion, courant):
    _, rows, second, cells = state_field.shape
    chunks = 4
    table = pltpu.with_memory_space_constraint(jnp.asarray(constant_table()), pltpu.HBM)
    state_in = pltpu.with_memory_space_constraint(state_field, pltpu.HBM)
    f32 = jnp.float32
    dma = pltpu.SemaphoreType.DMA
    hbm = lambda x: pltpu.with_memory_space_constraint(x, pltpu.HBM)
    small = [hbm(x) for x in (level_vectors, diffusion, courant)]
    smem = pl.BlockSpec(memory_space=pltpu.SMEM)
    anywhere = pl.BlockSpec(memory_space=pl.ANY)
    others = max(grids - 1, 1)
    own, far = pl.pallas_call(
        functools.partial(kernel, grids, doms, chunks),
        out_shape=[
            jax.ShapeDtypeStruct((rows, second, cells), f32),
            jax.ShapeDtypeStruct((2, second, cells), f32),
        ],
        in_specs=[smem] + [pl.BlockSpec(memory_space=pltpu.HBM)] * 5,
        out_specs=[anywhere] * 2,
        scratch_shapes=[
            pltpu.VMEM((rows, second, cells), f32),
            pltpu.VMEM((rows, second, cells), f32),
            pltpu.VMEM((rows, second, cells), f32),
            pltpu.VMEM((2, second, cells), f32),
            pltpu.VMEM((2, second, cells), f32),
            pltpu.VMEM(table.shape, jnp.bfloat16),
            pltpu.VMEM((2, 2, second, COARSE), f32),
            pltpu.VMEM((2, 2, second, COARSE), f32),
            pltpu.VMEM((rows * second, COARSE), f32),
            pltpu.VMEM((others, rows * second, COARSE), f32),
            pltpu.VMEM((SIDE * SIDE, rows * second, GROUP), f32),
            pltpu.SMEM(level_vectors.shape, jnp.int32),
            pltpu.SMEM(diffusion.shape, f32),
            pltpu.SMEM(courant.shape, f32),
            dma((5,)),
            dma((2,)),
            dma((2,)),
            dma((2, chunks)),
            dma((2, chunks)),
            dma((2,)),
            dma((2,)),
            dma((others,)),
            dma((others,)),
            dma((1,)),
        ],
        compiler_params=pltpu.CompilerParams(
            collective_id=0, has_side_effects=True, vmem_limit_bytes=40 * 2**20
        ),
    )(combine_weights, *small, state_in, table)
    if rows == 2:
        return (own + far)[None]
    parts = [own[:1] + far[:1], own[1:-1], own[-1:] + far[1:]]
    return jnp.concatenate(parts, axis=0)[None]


def solution(mesh):
    placed = (P("grid", "dom", None, None), P("grid", None), P("grid"), P(), P())
    return jax.shard_map(
        functools.partial(local, mesh.shape["grid"], mesh.shape["dom"]),
        mesh=mesh,
        in_specs=placed,
        out_specs=P("grid", "dom", None, None),
        check_vma=False,
    )
```
